32 devices in a mesh: rows: 8 (over z, y), seq: 4 (over x, core).
Axes of the slice: x: 2, y: 2, z: 4, core: 2. Of those that a mesh axis runs over, the one named last changes fastest.
Arguments:
- residual_in: bfloat16 [8, 2048, 3200], P('rows', 'seq'), may hold values from -6 to 6
- norm_gain: float32 [3200], replicated, may hold values from 0.1 to 1.9
- qkv_weight: bfloat16 [3200, 6144], P(None, 'seq')
- qk_gain: float32 [2, 2048], P(None, 'seq')
- out_weight: bfloat16 [2048, 3200], P('seq'), may hold values from -0.125 to 0.125
- layer_scale: float32 [3200], replicated, may hold values from 1 to 6
- segment_ids: int32 [8, 2048], P('rows', 'seq'), may hold values from 0 to 2, as said below
- pad_mask: int32 [8, 2048], P('rows', 'seq'), may hold values from 0 to 1, as said below
- ln_weight: float32 [12800], replicated, may hold values from 0.1 to 1.9
- ln_bias: float32 [12800], replicated, may hold values from -3 to 3
- fc_weight: bfloat16 [12800, 6144], P('rows'), may hold values from -0.0546875 to 0.0546875
- fc_bias: float32 [6144], replicated, may hold values from -3 to 3
- owner: int32 [8], replicated, may hold values from 0 to 7, each once
Outputs:
- features: bfloat16 [8, 512, 6144], P('rows', 'seq')
The draws below stay inside these ranges and needn't reach their ends.
Inputs may be any that keep to these rules, and one draw needn't show every extreme that they name: `segment_ids`: within a row, segment ids never fall and change only at multiples of 1024 tokens; picture tokens carry ids below 2, padding tokens carry 2 and stand at the end of the row; the first tile is never padding. pad_mask is 0 exactly where segment_ids equals 2. `owner`: each index of rows owns exactly one row.
All inputs are finite; a program needn't handle non-finite values.
Results may differ from the reference program's by a relative error of at most 0.025.
Values may be sent and summed in bfloat16 or wider, within the bound.
No kernel may reach another device: no remote copies, remote signals or barrier semaphores. Data moves between devices by JAX's collectives and lax.ppermute only.
A program may use at most 128 MiB of HBM per device.

```python
import math
import jax
import jax.numpy as jnp
from jax import lax

D = 3200
HEAD_DIM = 128
HID = 6144
HEADS = 16
GRID = 32
ROW_TOK = 2048
ROWS = 8
N_ROWS = 8
N_SEQ = 4


def packing(key):
    tile_count = ROW_TOK // (GRID * GRID)
    first_key = jax.random.fold_in(key, 11)
    second_key = jax.random.fold_in(key, 12)
    third_key = jax.random.fold_in(key, 13)
    cut_bits = jax.random.randint(first_key, (ROWS, tile_count), 0, 2)
    cut_bits = cut_bits.at[:, 0].set(0)
    picture = jnp.cumsum(cut_bits, axis=1)
    pad_tiles = jax.random.randint(second_key, (ROWS,), 0, tile_count)
    chosen = jax.random.randint(third_key, (), 0, ROWS)
    pad_tiles = jnp.where(jnp.arange(ROWS) == chosen, tile_count - 1, pad_tiles)
    tile_index = jnp.arange(tile_count)
    padded = tile_index[None, :] >= (tile_count - pad_tiles)[:, None]
    seg_tile = jnp.where(padded, tile_count, picture).astype(jnp.int32)
    valid = jnp.where(padded, 0, 1).astype(jnp.int32)
    return (jnp.repeat(seg_tile, GRID * GRID, axis=1), jnp.repeat(valid, GRID * GRID, axis=1))


def draw_segment_ids(key, part):
    return packing(key)[0]


def draw_pad_mask(key, part):
    return packing(key)[1]


def draw_qkv_weight(key, part):
    base_draw = jax.random.normal(jax.random.fold_in(key, 21), (D, HEADS, 3, HEAD_DIM), jnp.float32) * D ** (-0.5)
    head_scale = 3.0 ** (jnp.arange(HEADS, dtype=jnp.float32) / max(HEADS - 1, 1))
    wobble = jnp.exp(jax.random.uniform(jax.random.fold_in(key, 22), (HEADS,), jnp.float32, -0.2, 0.2))
    factor = jnp.stack([head_scale * wobble, head_scale * wobble, jnp.ones((HEADS,), jnp.float32)], axis=1)
    weights = base_draw * factor[None, :, :, None]
    return weights.reshape(D, HEADS * 3 * HEAD_DIM).astype(jnp.bfloat16)


def draw_qk_gain(key, part):
    gain_draw = jnp.exp(jax.random.uniform(jax.random.fold_in(key, 31), (2, HEADS, HEAD_DIM), jnp.float32, math.log(0.8), math.log(2.2)))
    return gain_draw.reshape(2, HEADS * HEAD_DIM)


def block_levels(own_key, shape, cuts, low, top_value):
    factor_of, own = 1.0, jax.random.fold_in(own_key, 6)
    for dim, shards_of in cuts:
        draws = jnp.exp(jax.random.uniform(jax.random.fold_in(own, dim), (shards_of,), jnp.float32, low / len(cuts), top_value / len(cuts)))
        factor_of = factor_of * jnp.repeat(draws, shape[dim] // shards_of).reshape([-1 if axis == dim else 1 for axis in range(len(shape))])
    return factor_of


def scatter_about(stream_key, dims, scale, limit, split=(), kind=jnp.bfloat16):
    array = scale * jax.random.normal(stream_key, dims, jnp.float32)
    if split:
        array = array * block_levels(stream_key, dims, split, -0.22, 0.18)
    return jnp.clip(array, -limit, limit).astype(kind)


def setup_inputs(seed: int = 0) -> dict:
    streams_of = jax.random.split(jax.random.key(seed), 14)
    return {
        "residual_in": scatter_about(streams_of[0], (ROWS, ROW_TOK, D), 1.0, 6.0, ((0, 8), (1, 4))),
        "norm_gain": jnp.clip(1.0 + 0.18 * jax.random.normal(streams_of[1], (D,), jnp.float32), 0.1, 1.9),
        "qkv_weight": draw_qkv_weight(jax.random.fold_in(streams_of[13], 71), 0),
        "qk_gain": draw_qk_gain(jax.random.fold_in(streams_of[13], 71), 0),
        "out_weight": scatter_about(streams_of[4], (HEADS * HEAD_DIM, D), (HEADS * HEAD_DIM) ** -0.5, 0.125, ((0, 4),)),
        "layer_scale": jnp.clip(jnp.exp(jax.random.uniform(streams_of[5], (D,), jnp.float32, math.log(1.0), math.log(6.0))), 1.0, 6.0),
        "segment_ids": draw_segment_ids(jax.random.fold_in(streams_of[13], 71), 0),
        "pad_mask": draw_pad_mask(jax.random.fold_in(streams_of[13], 71), 0),
        "ln_weight": jnp.clip(1.0 + 0.18 * jax.random.normal(streams_of[8], (4 * D,), jnp.float32), 0.1, 1.9),
        "ln_bias": scatter_about(streams_of[9], (4 * D,), 0.5, 3.0, (), jnp.float32),
        "fc_weight": scatter_about(streams_of[10], (4 * D, HID), (4 * D) ** -0.5, 0.0546875, ((0, 8),)),
        "fc_bias": scatter_about(streams_of[11], (HID,), 0.5, 3.0, (), jnp.float32),
        "owner": jax.random.permutation(streams_of[12], ROWS).astype(jnp.int32),
    }


def rounded_sum(left_parts, right_parts):

    def add_group(carry, pair):
        left, right = pair
        term = jnp.dot(left, right, preferred_element_type=jnp.float32).astype(jnp.bfloat16)
        term = lax.optimization_barrier(term)
        return (carry + term.astype(jnp.float32), None)
    start = jnp.zeros((left_parts.shape[1], right_parts.shape[2]), jnp.float32)
    result, _ = lax.scan(add_group, start, (left_parts, right_parts))
    return result

def reference(residual_in, norm_gain, qkv_weight, qk_gain, out_weight, layer_scale, segment_ids, pad_mask, ln_weight, ln_bias, fc_weight, fc_bias, owner):
    row_len = ROW_TOK
    norm_width = HEADS * HEAD_DIM
    group_width = norm_width // N_SEQ
    slab_width = 4 * D // N_ROWS
    half_grid = GRID // 2
    lines = row_len // (2 * GRID)
    scale = HEAD_DIM ** (-0.5)

    def one_row(packed):
        row_x, row_seg, row_mask = packed
        tokens = row_x.astype(jnp.float32)
        normed = (tokens * lax.rsqrt(lax.optimization_barrier(jnp.mean(tokens * tokens, axis=-1, keepdims=True)) + 1e-06) * norm_gain).astype(jnp.bfloat16)
        projected = jnp.dot(normed, qkv_weight, preferred_element_type=jnp.float32).reshape(row_len, HEADS, 3, HEAD_DIM)
        query_raw = projected[:, :, 0]
        key_raw = projected[:, :, 1]
        value_half = projected[:, :, 2].astype(jnp.bfloat16)
        query_gain = qk_gain[0].reshape(HEADS, HEAD_DIM)
        key_gain = qk_gain[1].reshape(HEADS, HEAD_DIM)
        query_norm = (query_raw * lax.rsqrt(lax.optimization_barrier(jnp.mean(query_raw * query_raw, axis=(1, 2))) + 1e-06)[:, None, None] * query_gain).astype(jnp.bfloat16)
        key_norm = (key_raw * lax.rsqrt(lax.optimization_barrier(jnp.mean(key_raw * key_raw, axis=(1, 2))) + 1e-06)[:, None, None] * key_gain).astype(jnp.bfloat16)
        same_seg = row_seg[:, None] == row_seg[None, :]

        def one_head(head):
            q_head = lax.dynamic_index_in_dim(query_norm, head, 1, keepdims=False)
            k_head = lax.dynamic_index_in_dim(key_norm, head, 1, keepdims=False)
            v_head = lax.dynamic_index_in_dim(value_half, head, 1, keepdims=False)
            scores = jnp.dot(q_head, k_head.T, preferred_element_type=jnp.float32) * scale
            scores = jnp.where(same_seg, scores, -1e+30)
            peak_val = lax.optimization_barrier(jnp.max(scores, axis=-1, keepdims=True))
            exp_terms = jnp.exp(scores - peak_val)
            probs = (exp_terms / lax.optimization_barrier(jnp.sum(exp_terms, axis=-1, keepdims=True))).astype(jnp.bfloat16)
            return jnp.dot(probs, v_head, preferred_element_type=jnp.float32).astype(jnp.bfloat16)
        heads_out = lax.map(one_head, jnp.arange(HEADS, dtype=jnp.int32))
        heads_out = jnp.transpose(heads_out, (1, 0, 2)).reshape(row_len, norm_width)
        attn = rounded_sum(jnp.transpose(heads_out.reshape(row_len, N_SEQ, group_width), (1, 0, 2)), out_weight.reshape(N_SEQ, group_width, D))
        hidden = tokens + layer_scale * attn
        merged = jnp.transpose(hidden.reshape(lines, 2, half_grid, 2, D), (0, 2, 1, 3, 4)).reshape(row_len // 4, 4 * D)
        centre = merged - lax.optimization_barrier(jnp.mean(merged, axis=-1, keepdims=True))
        spread = lax.optimization_barrier(jnp.mean(centre * centre, axis=-1, keepdims=True))
        merged_norm = (centre * lax.rsqrt(spread + 1e-05) * ln_weight + ln_bias).astype(jnp.bfloat16)
        pre = rounded_sum(jnp.transpose(merged_norm.reshape(row_len // 4, N_ROWS, slab_width), (1, 0, 2)), fc_weight.reshape(N_ROWS, slab_width, HID)) + fc_bias
        merged_mask = row_mask.reshape(lines, 2, half_grid, 2)[:, 0, :, 0].reshape(row_len // 4).astype(jnp.float32)
        return (jax.nn.gelu(pre, approximate=False) * merged_mask[:, None]).astype(jnp.bfloat16)
    results = lax.map(one_row, (residual_in, segment_ids, pad_mask))
    return jnp.zeros_like(results).at[owner].set(results)
```

```python
import functools
import math

import jax
import jax.numpy as jnp
import numpy as np
from jax import lax
from jax.experimental import pallas as pl
from jax.experimental.pallas import tpu as pltpu
from jax.sharding import PartitionSpec as P

D = 3200
HEAD_DIM = 128
HEADS = 16
GRID = 32
TILE = GRID * GRID
SUBS = 4
CHUNKS = 2
HALVES = 2
MIB = 1024 * 1024
BF16 = jnp.bfloat16
F32 = jnp.float32


def reorder_kernel(pick_ref, x_ref, out_ref):
    out_ref[...] = jnp.dot(pick_ref[...], x_ref[...], preferred_element_type=F32).astype(BF16)


def reorder(x, chunk):
    lines = chunk // (2 * GRID)
    source = np.arange(chunk).reshape(lines, 2, GRID // 2, 2).transpose(1, 3, 0, 2).reshape(chunk)
    pick = jnp.asarray(np.eye(chunk, dtype=np.float32)[source], BF16)
    return pl.pallas_call(
        reorder_kernel,
        grid=(x.shape[0] // chunk,),
        in_specs=[
            pl.BlockSpec((chunk, chunk), lambda i: (0, 0)),
            pl.BlockSpec((chunk, D), lambda i: (i, 0)),
        ],
        out_specs=pl.BlockSpec((chunk, D), lambda i: (i, 0)),
        out_shape=jax.ShapeDtypeStruct(x.shape, BF16),
        cost_estimate=pl.CostEstimate(
            flops=2 * x.shape[0] * chunk * D, bytes_accessed=4 * x.size, transcendentals=0
        ),
        compiler_params=pltpu.CompilerParams(vmem_limit_bytes=32 * MIB),
        name="reorder",
    )(pick, x)


def qkv_kernel(count, *refs):
    x_refs, gain_ref, w_ref = refs[:count], refs[count], refs[count + 1]
    out_refs = refs[count + 2 : 2 * count + 2]
    sq_refs = refs[2 * count + 2 : 3 * count + 2]
    normed, q_acc, k_acc = refs[3 * count + 2 :]
    head = pl.program_id(0)
    rows = x_refs[0].shape[0]
    step = 64

    @pl.when(head == 0)
    def _():
        for i in range(count):

            @pl.loop(0, rows // step)
            def _(b):
                part = pl.ds(pl.multiple_of(b * step, step), step)
                x = x_refs[i][part, :].astype(F32)
                inv = lax.rsqrt(jnp.mean(x * x, axis=-1, keepdims=True) + 1e-06)
                normed[i, part, :] = (x * inv * gain_ref[...]).astype(BF16)

        q_acc[...] = jnp.zeros_like(q_acc)
        k_acc[...] = jnp.zeros_like(k_acc)

    for i in range(count):
        product = jnp.dot(normed[i], w_ref[...], preferred_element_type=F32)
        out_refs[i][...] = product
        for first in range(0, product.shape[1], 3 * HEAD_DIM):
            q = product[:, first : first + HEAD_DIM]
            k = product[:, first + HEAD_DIM : first + 2 * HEAD_DIM]
            q_acc[i] += q * q
            k_acc[i] += k * k

    @pl.when(head == pl.num_programs(0) - 1)
    def _():
        for i in range(count):
            sq_refs[i][0:1, :] = jnp.sum(q_acc[i].T, axis=0, keepdims=True)
            sq_refs[i][1:2, :] = jnp.sum(k_acc[i].T, axis=0, keepdims=True)


def project(pieces, norm_gain, qkv_weight):
    count = len(pieces)
    rows = pieces[0].shape[0]
    width = qkv_weight.shape[1]
    heads = width // (3 * HEAD_DIM)
    block = 3 * HEAD_DIM * (2 if heads % 2 == 0 else 1)
    results = pl.pallas_call(
        functools.partial(qkv_kernel, count),
        grid=(width // block,),
        in_specs=[pl.BlockSpec((rows, D), lambda h: (0, 0))] * count
        + [
            pl.BlockSpec((1, D), lambda h: (0, 0)),
            pl.BlockSpec((D, block), lambda h: (0, h)),
        ],
        out_specs=[pl.BlockSpec((rows, block), lambda h: (0, h))] * count
        + [pl.BlockSpec((2, rows), lambda h: (0, 0))] * count,
        out_shape=[jax.ShapeDtypeStruct((rows, width), F32)] * count
        + [jax.ShapeDtypeStruct((2, rows), F32)] * count,
        scratch_shapes=[
            pltpu.VMEM((count, rows, D), BF16),
            pltpu.VMEM((count, rows, HEAD_DIM), F32),
            pltpu.VMEM((count, rows, HEAD_DIM), F32),
        ],
        cost_estimate=pl.CostEstimate(
            flops=2 * count * rows * D * width,
            bytes_accessed=2 * D * width + count * rows * (2 * D + 4 * width),
            transcendentals=0,
        ),
        compiler_params=pltpu.CompilerParams(vmem_limit_bytes=56 * MIB),
        name="qkv",
    )(*pieces, norm_gain.reshape(1, D), qkv_weight)
    return results[:count], results[count:]


def attend_kernel(plan, rows, first, chunk, group, *refs):
    count = len(plan)
    blocks = plan[-1][0] + 1
    seg_ref, sq_ref, gain_ref = refs[:3]
    p_refs = refs[3 : 3 + count]
    out_ref, q_scale, k_scale, q_all, k_all, v_all = refs[3 + count :]
    head = pl.program_id(0)
    factor = HEAD_DIM ** (-0.5) * math.log2(math.e)

    @pl.when(head == 0)
    def _():
        inv = lax.rsqrt(sq_ref[...] / (HEADS * HEAD_DIM) + 1e-06)
        for d in range(blocks):
            part = slice(d * rows, (d + 1) * rows)
            k_scale[part, :] = jnp.broadcast_to(inv[1:2, part], (HEAD_DIM, rows)).T
            q_wide = jnp.broadcast_to(inv[0:1, part] * factor, (HEAD_DIM, rows)).T
            q_scale[d * chunk : (d + 1) * chunk, :] = q_wide[first : first + chunk, :]
        v_all[:, HEAD_DIM:] = jnp.ones_like(v_all[:, HEAD_DIM:])

    for (d, start, size), p_ref in zip(plan, p_refs):
        part = slice(d * rows + start, d * rows + start + size)
        k = p_ref[:, HEAD_DIM : 2 * HEAD_DIM]
        k_all[part, :] = (k * k_scale[part, :] * gain_ref[1:2, :]).astype(BF16)
        v_all[part, :HEAD_DIM] = p_ref[:, 2 * HEAD_DIM :].astype(BF16)
        low, high = max(first, start), min(first + chunk, start + size)
        if low < high:
            part = slice(d * chunk + low - first, d * chunk + high - first)
            q = p_ref[low - start : high - start, :HEAD_DIM]
            q_all[part, :] = (q * q_scale[part, :] * gain_ref[0:1, :]).astype(BF16)

    groups = blocks // group
    keys = group * rows
    step = min(chunk, 128)

    def attend(d, begin, low, high):
        q = q_all[d * chunk + begin : d * chunk + begin + step, :]
        scores = lax.dot_general(
            q, k_all[low:high, :], (((1,), (1,)), ((), ())), preferred_element_type=F32
        )
        if groups > 2:
            own = d // group
            masked = []
            for g in range(groups):
                part = scores[:, g * keys : (g + 1) * keys]
                if g != own:
                    part = jnp.where(seg_ref[g] == seg_ref[own], part, -1e30)
                masked.append(part)
            scores = jnp.concatenate(masked, axis=1)
        peak = jnp.max(scores, axis=-1, keepdims=True)
        terms = jnp.exp2(scores - peak).astype(BF16)
        both = jnp.dot(terms, v_all[low:high, :], preferred_element_type=F32)
        out_ref[d, begin : begin + step, :] = (
            both[:, :HEAD_DIM] / both[:, HEAD_DIM:]
        ).astype(BF16)

    def attend_all(d, low, high):
        for begin in range(0, chunk, step):
            attend(d, begin, low, high)

    if groups != 2:
        for d in range(blocks):
            attend_all(d, 0, blocks * rows)
    else:
        joint = seg_ref[0] == seg_ref[1]

        @pl.when(joint)
        def _():
            for d in range(blocks):
                attend_all(d, 0, blocks * rows)

        @pl.when(jnp.logical_not(joint))
        def _():
            for d in range(blocks):
                own = d // group
                attend_all(d, own * keys, (own + 1) * keys)


def attend(pieces, plan, rows, squares, segments, qk_gain, first, chunk):
    blocks = plan[-1][0] + 1
    width = pieces[0].shape[1]
    heads = width // (3 * HEAD_DIM)
    total = blocks * rows
    group = max(1, min(blocks, TILE // rows))
    return pl.pallas_call(
        functools.partial(attend_kernel, plan, rows, first, chunk, group),
        grid=(heads,),
        in_specs=[
            pl.BlockSpec(memory_space=pltpu.SMEM),
            pl.BlockSpec((2, total), lambda h: (0, 0)),
            pl.BlockSpec((2, HEAD_DIM), lambda h: (0, h)),
        ]
        + [pl.BlockSpec((size, 3 * HEAD_DIM), lambda h: (0, h)) for _, _, size in plan],
        out_specs=pl.BlockSpec((blocks, chunk, HEAD_DIM), lambda h: (0, 0, h)),
        out_shape=jax.ShapeDtypeStruct((blocks, chunk, heads * HEAD_DIM), BF16),
        scratch_shapes=[
            pltpu.VMEM((blocks * chunk, HEAD_DIM), F32),
            pltpu.VMEM((total, HEAD_DIM), F32),
            pltpu.VMEM((blocks * chunk, HEAD_DIM), BF16),
            pltpu.VMEM((total, HEAD_DIM), BF16),
            pltpu.VMEM((total, 2 * HEAD_DIM), BF16),
        ],
        cost_estimate=pl.CostEstimate(
            flops=8 * heads * blocks * chunk * total * HEAD_DIM,
            bytes_accessed=4 * total * width,
            transcendentals=heads * blocks * chunk * total,
        ),
        compiler_params=pltpu.CompilerParams(vmem_limit_bytes=56 * MIB),
        name="attend",
    )(segments, squares, qk_gain, *pieces)


def per_device(
    residual_in,
    norm_gain,
    qkv_weight,
    qk_gain,
    out_weight,
    layer_scale,
    segment_ids,
    pad_mask,
    ln_weight,
    ln_bias,
    fc_weight,
    fc_bias,
    owner,
):
    x = residual_in[0]
    rows_here = x.shape[0]
    n_seq, n_rows = lax.axis_size("seq"), lax.axis_size("rows")
    row = lax.axis_index("rows")
    parts = n_rows // SUBS
    sub, part = row // parts, row % parts
    width = D // parts
    chunk = rows_here // CHUNKS
    merged = chunk // SUBS
    hid = fc_weight.shape[1]

    def over_seq(value, d):
        return lax.ppermute(value, "seq", [(i, i ^ d) for i in range(n_seq)])

    def over_sub(value, d):
        return lax.ppermute(value, "rows", [(i, i ^ (d * parts)) for i in range(n_rows)])

    def over_part(value, d):
        return lax.ppermute(value, "rows", [(i, i ^ d) for i in range(n_rows)])

    def spread(value, axis):
        count = 1
        while count < lax.axis_size(axis):
            steps = [(i, i ^ count) for i in range(lax.axis_size(axis))]
            value = jnp.concatenate([value, lax.ppermute(value, axis, steps)])
            count *= 2
        return value

    def pick(value, index, axis=0):
        return lax.dynamic_index_in_dim(value, index, axis, keepdims=False)

    fence = lax.optimization_barrier

    tokens = reorder(x, chunk)
    cuts = [0, rows_here * 3 // 4, rows_here]
    cut = [tokens[low:high] for low, high in zip(cuts, cuts[1:])]
    by_sub = tokens.reshape(CHUNKS, SUBS, merged, D)
    residual = {0: pick(by_sub, sub, 1)}
    to_send = {d: pick(by_sub, sub ^ d, 1) for d in range(1, SUBS)}
    share = out_weight.shape[0] // n_rows
    strip = lax.dynamic_slice_in_dim(out_weight, row * share, share, 0)
    group = max(1, min(n_seq, TILE // rows_here))
    projected, squares = {}, {}

    far = {d: over_seq(cut[0], d) for d in range(2, n_seq, 2)}
    near = over_seq(tokens, 1)
    strips = {d: over_seq(strip, d) for d in range(2, n_seq, 2)}
    for d in (1, 2):
        residual[d] = over_sub(to_send[d], d)
    given, given_s = project([tokens, near], norm_gain, qkv_weight)
    for d in range(2):
        projected[d, 0], squares[d, 0] = given[d], given_s[d]
    state = far, cut[1], strips, residual, to_send, squares, segment_ids, pad_mask, out_weight
    far, later, strips, residual, to_send, squares, segment_ids, pad_mask, out_weight = fence(state)

    coming = {d: over_seq(later, d) for d in range(2, n_seq, 2)}
    out_blocks = {0: out_weight, 1: over_seq(out_weight, 1)}
    for d in range(2, n_seq, 2):
        out_blocks[d] = lax.all_gather(strips[d], "rows", axis=0, tiled=True)
        far[d + 1] = over_seq(far[d], 1)
    for d in range(3, SUBS):
        residual[d] = over_sub(to_send[d], d)
    leads = spread(segment_ids[0, :1], "seq")[::group]
    masks = spread(pad_mask[0, :1], "rows")
    given, given_s = project([far[d] for d in range(2, n_seq)], norm_gain, qkv_weight)
    for d in range(2, n_seq):
        projected[d, 0], squares[d, 0] = given[d - 2], given_s[d - 2]
    far, residual, squares, leads, masks = fence((coming, residual, squares, leads, masks))

    for d in range(2, n_seq, 2):
        far[d + 1] = over_seq(far[d], 1)
    given, given_s = project([far[d] for d in range(2, n_seq)], norm_gain, qkv_weight)
    for d in range(2, n_seq):
        projected[d, 1], squares[d, 1] = given[d - 2], given_s[d - 2]
    plan, pieces = [], []
    for d, i in sorted(projected):
        plan.append((d, cuts[i], projected[d, i].shape[0]))
        pieces.append(projected[d, i])

    here = jnp.concatenate([squares[key] for key in sorted(squares)], axis=1)
    here = jnp.transpose(here.reshape(2, n_seq, rows_here), (1, 0, 2))
    total = here
    for e in range(1, n_seq):
        there = over_seq(here, e)
        total = total + jnp.stack([there[d ^ e] for d in range(n_seq)])
    total = jnp.transpose(total, (1, 0, 2)).reshape(2, n_seq * rows_here)

    for d in range(2, n_seq, 2):
        out_blocks[d + 1] = over_seq(out_blocks[d], 1)
    out_full = jnp.concatenate([out_blocks[d] for d in range(n_seq)], axis=0)

    sub_ln = lax.dynamic_slice_in_dim(ln_weight, sub * D, D, 0)
    sub_bias = lax.dynamic_slice_in_dim(ln_bias, sub * D, D, 0)
    source = jnp.argmax(owner[None, :] == jnp.arange(n_rows, dtype=jnp.int32)[:, None], axis=1)
    own_mask = pick(masks, pick(source, row) ^ row).astype(F32)
    wanted = []
    for f in range(parts):
        for g in range(SUBS):
            p = pick(source, (sub ^ g) * parts + (part ^ f))
            wanted.append((p % parts ^ part) * SUBS + (p // parts ^ sub))
    wanted_hot = (
        jnp.stack(wanted)[:, None] == jnp.arange(n_rows, dtype=jnp.int32)[None, :]
    ).astype(BF16)

    def heads_of(j, sums):
        return attend(pieces, plan, rows_here, sums, leads, qk_gain, j * chunk, chunk)

    def gather_rows(heads):
        groups = [heads[0]] + [over_seq(heads[d], d) for d in range(1, n_seq)]
        heads = jnp.concatenate(groups, axis=-1).reshape(SUBS, merged, HEADS * HEAD_DIM)
        mine = [pick(heads, sub)]
        for d in range(1, SUBS):
            mine.append(over_sub(pick(heads, sub ^ d), d))
        return jnp.concatenate(mine, axis=0)

    def to_slab(j, mine):
        attn = jnp.dot(mine, out_full, preferred_element_type=F32)
        stream = jnp.concatenate([residual[d][j] for d in range(SUBS)], axis=0).astype(F32)
        hidden = stream + layer_scale * attn
        mean_here = jnp.mean(hidden, axis=-1)
        centre = hidden - mean_here[:, None]
        spread_here = jnp.sum(centre * centre, axis=-1)
        stats = jnp.stack([mean_here, spread_here]).reshape(2, SUBS, merged)
        known = [stats]
        for e in range(1, SUBS):
            there = over_sub(stats, e)
            known.append(jnp.stack([there[:, d ^ e] for d in range(SUBS)], axis=1))
        mean = sum(k[0] for k in known) / SUBS
        var = sum(k[1] + D * (k[0] - mean) * (k[0] - mean) for k in known) / (SUBS * D)
        mean, var = mean.reshape(-1, 1), var.reshape(-1, 1)
        normed = (
            (hidden - mean) * lax.rsqrt(var + 1e-05) * sub_ln + sub_bias
        ).astype(BF16)
        by_part = jnp.stack([normed[:, i * width : (i + 1) * width] for i in range(parts)])
        slab = [pick(by_part, part)]
        for e in range(1, parts):
            slab.append(over_part(pick(by_part, part ^ e), e))
        return jnp.concatenate(slab, axis=0)

    def to_shares(slab):
        half = merged // HALVES
        ordered = jnp.einsum(
            "jp,phms->hjms",
            wanted_hot,
            slab.reshape(n_rows, HALVES, half, width),
            preferred_element_type=F32,
        ).astype(BF16)
        shares = jnp.dot(
            ordered.reshape(n_rows * merged, width), fc_weight, preferred_element_type=F32
        ).astype(BF16)
        return shares.reshape(HALVES, parts, SUBS, half, hid)

    def sum_parts(shares):
        summed = shares[0].astype(F32)
        for e in range(1, parts):
            summed = summed + over_part(shares[e], e).astype(F32)
        return summed.astype(BF16)

    def sum_subs(summed):
        pre = summed[0].astype(F32)
        for d in range(1, SUBS):
            pre = pre + over_sub(summed[d], d).astype(F32)
        return pre

    def finish(pre):
        return (jax.nn.gelu(pre + fc_bias, approximate=False) * own_mask).astype(BF16)

    heads, rows, slab, shares, summed, pre, outs = {}, {}, {}, {}, {}, {}, {}
    state = total, heads, rows, slab, shares, summed, pre, outs
    units = [(j, h) for j in range(CHUNKS) for h in range(HALVES)]
    for tick in range(3 + CHUNKS + len(units) + 1):
        total, heads, rows, slab, shares, summed, pre, outs = state
        new = total, {}, {}, {}, dict(shares), {}, {}, dict(outs)
        if tick < CHUNKS:
            new[1][tick] = heads_of(tick, total)
        for j in heads:
            new[2][j] = gather_rows(heads[j])
        for j in rows:
            new[3][j] = to_slab(j, rows[j])
        for j in slab:
            given = to_shares(slab[j])
            new[4].update({(j, h): given[h] for h in range(HALVES)})
        if shares:
            unit = min(shares)
            new[5][unit] = sum_parts(new[4].pop(unit))
        for unit in summed:
            new[6][unit] = sum_subs(summed[unit])
        for unit in pre:
            new[7][unit] = finish(pre[unit])
        state = fence(new)
    outs = state[-1]
    return jnp.concatenate([outs[unit] for unit in units], axis=0)[None]


def solution(mesh):
    return jax.shard_map(
        per_device,
        mesh=mesh,
        in_specs=(
            P("rows", "seq", None),
            P(),
            P(None, "seq"),
            P(None, "seq"),
            P("seq", None),
            P(),
            P("rows", "seq"),
            P("rows", "seq"),
            P(),
            P(),
            P("rows", None),
            P(),
            P(),
        ),
        out_specs=P("rows", "seq", None),
        check_vma=False,
    )
```

```python
import functools
import math

import jax
import jax.numpy as jnp
import numpy as np
from jax import lax
from jax.experimental import pallas as pl
from jax.experimental.pallas import tpu as pltpu
from jax.sharding import PartitionSpec as P

D = 3200
HEAD_DIM = 128
HEADS = 16
GRID = 32
TILE = GRID * GRID
SUBS = 4
CHUNKS = 2
HALVES = 2
MIB = 1024 * 1024
BF16 = jnp.bfloat16
F32 = jnp.float32
TINY = pl.CostEstimate(flops=1, bytes_accessed=1, transcendentals=0)


def reorder_kernel(pick_ref, x_ref, out_ref):
    out_ref[...] = jnp.dot(pick_ref[...], x_ref[...], preferred_element_type=F32).astype(BF16)


def reorder(x, chunk):
    lines = chunk // (2 * GRID)
    source = np.arange(chunk).reshape(lines, 2, GRID // 2, 2).transpose(1, 3, 0, 2).reshape(chunk)
    pick = jnp.asarray(np.eye(chunk, dtype=np.float32)[source], BF16)
    return pl.pallas_call(
        reorder_kernel,
        grid=(x.shape[0] // chunk,),
        in_specs=[
            pl.BlockSpec((chunk, chunk), lambda i: (0, 0)),
            pl.BlockSpec((chunk, D), lambda i: (i, 0)),
        ],
        out_specs=pl.BlockSpec((chunk, D), lambda i: (i, 0)),
        out_shape=jax.ShapeDtypeStruct(x.shape, BF16),
        cost_estimate=pl.CostEstimate(
            flops=2 * x.shape[0] * chunk * D, bytes_accessed=4 * x.size, transcendentals=0
        ),
        compiler_params=pltpu.CompilerParams(vmem_limit_bytes=32 * MIB),
        name="reorder",
    )(pick, x)


def qkv_kernel(count, *refs):
    x_refs, gain_ref, w_ref = refs[:count], refs[count], refs[count + 1]
    out_refs = refs[count + 2 : 2 * count + 2]
    sq_refs = refs[2 * count + 2 : 3 * count + 2]
    normed, q_acc, k_acc = refs[3 * count + 2 :]
    head = pl.program_id(0)
    rows = x_refs[0].shape[0]
    step = 64

    @pl.when(head == 0)
    def _():
        for i in range(count):

            @pl.loop(0, rows // step)
            def _(b):
                part = pl.ds(pl.multiple_of(b * step, step), step)
                x = x_refs[i][part, :].astype(F32)
                inv = lax.rsqrt(jnp.mean(x * x, axis=-1, keepdims=True) + 1e-06)
                normed[i, part, :] = (x * inv * gain_ref[...]).astype(BF16)

        q_acc[...] = jnp.zeros_like(q_acc)
        k_acc[...] = jnp.zeros_like(k_acc)

    for i in range(count):
        product = jnp.dot(normed[i], w_ref[...], preferred_element_type=F32)
        out_refs[i][...] = product
        for first in range(0, product.shape[1], 3 * HEAD_DIM):
            q = product[:, first : first + HEAD_DIM]
            k = product[:, first + HEAD_DIM : first + 2 * HEAD_DIM]
            q_acc[i] += q * q
            k_acc[i] += k * k

    @pl.when(head == pl.num_programs(0) - 1)
    def _():
        for i in range(count):
            sq_refs[i][0:1, :] = jnp.sum(q_acc[i].T, axis=0, keepdims=True)
            sq_refs[i][1:2, :] = jnp.sum(k_acc[i].T, axis=0, keepdims=True)


def project(pieces, norm_gain, qkv_weight):
    count = len(pieces)
    rows = pieces[0].shape[0]
    width = qkv_weight.shape[1]
    heads = width // (3 * HEAD_DIM)
    block = 3 * HEAD_DIM * (2 if heads % 2 == 0 else 1)
    results = pl.pallas_call(
        functools.partial(qkv_kernel, count),
        grid=(width // block,),
        in_specs=[pl.BlockSpec((rows, D), lambda h: (0, 0))] * count
        + [
            pl.BlockSpec((1, D), lambda h: (0, 0)),
            pl.BlockSpec((D, block), lambda h: (0, h)),
        ],
        out_specs=[pl.BlockSpec((rows, block), lambda h: (0, h))] * count
        + [pl.BlockSpec((2, rows), lambda h: (0, 0))] * count,
        out_shape=[jax.ShapeDtypeStruct((rows, width), F32)] * count
        + [jax.ShapeDtypeStruct((2, rows), F32)] * count,
        scratch_shapes=[
            pltpu.VMEM((count, rows, D), BF16),
            pltpu.VMEM((count, rows, HEAD_DIM), F32),
            pltpu.VMEM((count, rows, HEAD_DIM), F32),
        ],
        cost_estimate=TINY,
        compiler_params=pltpu.CompilerParams(vmem_limit_bytes=56 * MIB),
        name="qkv",
    )(*pieces, norm_gain.reshape(1, D), qkv_weight)
    return results[:count], results[count:]


def attend_kernel(plan, rows, first, chunk, group, *refs):
    count = len(plan)
    blocks = plan[-1][0] + 1
    seg_ref, sq_ref, gain_ref = refs[:3]
    p_refs = refs[3 : 3 + count]
    out_refs = refs[3 + count : 3 + count + blocks]
    q_scale, k_scale, q_all, k_all, v_all = refs[3 + count + blocks :]
    head = pl.program_id(0)
    factor = HEAD_DIM ** (-0.5) * math.log2(math.e)

    @pl.when(head == 0)
    def _():
        inv = lax.rsqrt(sq_ref[...] / (HEADS * HEAD_DIM) + 1e-06)
        for d in range(blocks):
            part = slice(d * rows, (d + 1) * rows)
            k_scale[part, :] = jnp.broadcast_to(inv[1:2, part], (HEAD_DIM, rows)).T
            q_wide = jnp.broadcast_to(inv[0:1, part] * factor, (HEAD_DIM, rows)).T
            q_scale[d * chunk : (d + 1) * chunk, :] = q_wide[first : first + chunk, :]
        v_all[:, HEAD_DIM:] = jnp.ones_like(v_all[:, HEAD_DIM:])

    for (d, start, size), p_ref in zip(plan, p_refs):
        part = slice(d * rows + start, d * rows + start + size)
        k = p_ref[:, HEAD_DIM : 2 * HEAD_DIM]
        k_all[part, :] = (k * k_scale[part, :] * gain_ref[1:2, :]).astype(BF16)
        v_all[part, :HEAD_DIM] = p_ref[:, 2 * HEAD_DIM :].astype(BF16)
        low, high = max(first, start), min(first + chunk, start + size)
        if low < high:
            part = slice(d * chunk + low - first, d * chunk + high - first)
            q = p_ref[low - start : high - start, :HEAD_DIM]
            q_all[part, :] = (q * q_scale[part, :] * gain_ref[0:1, :]).astype(BF16)

    groups = blocks // group
    keys = group * rows
    step = min(chunk, 128)

    def attend(d, begin, low, high):
        q = q_all[d * chunk + begin : d * chunk + begin + step, :]
        scores = lax.dot_general(
            q, k_all[low:high, :], (((1,), (1,)), ((), ())), preferred_element_type=F32
        )
        if groups > 2:
            own = d // group
            masked = []
            for g in range(groups):
                part = scores[:, g * keys : (g + 1) * keys]
                if g != own:
                    part = jnp.where(seg_ref[g] == seg_ref[own], part, -1e30)
                masked.append(part)
            scores = jnp.concatenate(masked, axis=1)
        peak = jnp.max(scores, axis=-1, keepdims=True)
        terms = jnp.exp2(scores - peak).astype(BF16)
        both = jnp.dot(terms, v_all[low:high, :], preferred_element_type=F32)
        out_refs[d][begin : begin + step, :] = (
            both[:, :HEAD_DIM] / both[:, HEAD_DIM:]
        ).astype(BF16)

    def attend_all(d, low, high):
        for begin in range(0, chunk, step):
            attend(d, begin, low, high)

    if groups != 2:
        for d in range(blocks):
            attend_all(d, 0, blocks * rows)
    else:
        joint = seg_ref[0] == seg_ref[1]

        @pl.when(joint)
        def _():
            for d in range(blocks):
                attend_all(d, 0, blocks * rows)

        @pl.when(jnp.logical_not(joint))
        def _():
            for d in range(blocks):
                own = d // group
                attend_all(d, own * keys, (own + 1) * keys)


def attend(pieces, plan, rows, squares, segments, qk_gain, first, chunk):
    blocks = plan[-1][0] + 1
    width = pieces[0].shape[1]
    heads = width // (3 * HEAD_DIM)
    total = blocks * rows
    group = max(1, min(blocks, TILE // rows))
    return pl.pallas_call(
        functools.partial(attend_kernel, plan, rows, first, chunk, group),
        grid=(heads,),
        in_specs=[
            pl.BlockSpec(memory_space=pltpu.SMEM),
            pl.BlockSpec((2, total), lambda h: (0, 0)),
            pl.BlockSpec((2, HEAD_DIM), lambda h: (0, h)),
        ]
        + [pl.BlockSpec((size, 3 * HEAD_DIM), lambda h: (0, h)) for _, _, size in plan],
        out_specs=[pl.BlockSpec((chunk, HEAD_DIM), lambda h: (0, h))] * blocks,
        out_shape=[jax.ShapeDtypeStruct((chunk, heads * HEAD_DIM), BF16)] * blocks,
        scratch_shapes=[
            pltpu.VMEM((blocks * chunk, HEAD_DIM), F32),
            pltpu.VMEM((total, HEAD_DIM), F32),
            pltpu.VMEM((blocks * chunk, HEAD_DIM), BF16),
            pltpu.VMEM((total, HEAD_DIM), BF16),
            pltpu.VMEM((total, 2 * HEAD_DIM), BF16),
        ],
        cost_estimate=TINY,
        compiler_params=pltpu.CompilerParams(vmem_limit_bytes=56 * MIB),
        name="attend",
    )(segments, squares, qk_gain, *pieces)


def pack_kernel(sub_ref, *refs):
    outs = refs[-SUBS:]
    rows, width = outs[0].shape[0], refs[0].shape[1]
    for d in range(SUBS):
        part = pl.ds(pl.multiple_of((sub_ref[0] ^ d) * rows, rows), rows)
        for i, ref in enumerate(refs[:-SUBS]):
            outs[d][:, i * width : (i + 1) * width] = ref[part, :]


def pack(groups, sub):
    chunk, width = groups[0].shape
    shape = (chunk // SUBS, width * len(groups))
    vmem = pl.BlockSpec(memory_space=pltpu.VMEM)
    return pl.pallas_call(
        pack_kernel,
        in_specs=[pl.BlockSpec(memory_space=pltpu.SMEM)] + [vmem] * len(groups),
        out_specs=[vmem] * SUBS,
        out_shape=[jax.ShapeDtypeStruct(shape, BF16)] * SUBS,
        compiler_params=pltpu.CompilerParams(vmem_limit_bytes=32 * MIB),
        name="pack",
    )(sub.reshape(1), *groups)


def hidden_kernel(count, mask_ref, *refs):
    mine_refs, stream_refs = refs[:SUBS], refs[SUBS : 2 * SUBS]
    w_refs = refs[2 * SUBS : 2 * SUBS + count]
    scale_ref, hidden_ref, stats_ref, mine, mean_wide, spread_wide = refs[2 * SUBS + count :]
    rows = mine_refs[0].shape[0]
    depth, block = w_refs[0].shape
    n = pl.program_id(0)

    @pl.when(n == 0)
    def _():
        for d in range(SUBS):
            mine[d * rows : (d + 1) * rows, :] = mine_refs[d][...]

    attn = jnp.dot(mine[:, :depth], w_refs[0][...], preferred_element_type=F32)
    for i in range(1, count):
        attn += jnp.dot(
            mine[:, i * depth : (i + 1) * depth], w_refs[i][...], preferred_element_type=F32
        )
    columns = pl.ds(pl.multiple_of(n * block, block), block)
    for d in range(SUBS):
        part = slice(d * rows, (d + 1) * rows)
        stream = stream_refs[d][0].astype(F32)
        hidden_ref[part, columns] = stream + scale_ref[...] * attn[part, :]

    @pl.when(n == pl.num_programs(0) - 1)
    def _():
        for d in range(SUBS):
            part = slice(d * rows, (d + 1) * rows)
            hidden = hidden_ref[part, :]
            mean = jnp.sum(hidden, axis=-1, keepdims=True) / D
            centre = hidden - mean
            spread = jnp.sum(centre * centre, axis=-1, keepdims=True)
            mean_wide[part, :] = jnp.broadcast_to(mean, (rows, 128))
            spread_wide[part, :] = jnp.broadcast_to(spread, (rows, 128))
        stats_ref[0:1, :] = mean_wide[...].T[0:1, :]
        stats_ref[1:2, :] = spread_wide[...].T[0:1, :]
        stats_ref[2:3, :] = jnp.full((1, SUBS * rows), mask_ref[0].astype(F32))


def hidden_of(places, mine, residual, weights, layer_scale, mask):
    rows = mine[0].shape[0]
    count, depth, block = len(weights), weights[0].shape[0], 640
    total = SUBS * rows
    return pl.pallas_call(
        functools.partial(hidden_kernel, count),
        grid=(D // block,),
        in_specs=[pl.BlockSpec(memory_space=pltpu.SMEM)]
        + [pl.BlockSpec(mine[0].shape, lambda n: (0, 0))] * SUBS
        + [pl.BlockSpec((1, rows, block), lambda n, j=j: (j, 0, n)) for j in places]
        + [pl.BlockSpec((depth, block), lambda n: (0, n))] * count
        + [pl.BlockSpec((1, block), lambda n: (0, n))],
        out_specs=[
            pl.BlockSpec((total, D), lambda n: (0, 0)),
            pl.BlockSpec((3, total), lambda n: (0, 0)),
        ],
        out_shape=[
            jax.ShapeDtypeStruct((total, D), F32),
            jax.ShapeDtypeStruct((3, total), F32),
        ],
        scratch_shapes=[
            pltpu.VMEM((total, count * depth), BF16),
            pltpu.VMEM((total, 128), F32),
            pltpu.VMEM((total, 128), F32),
        ],
        cost_estimate=pl.CostEstimate(
            flops=2 * total * count * depth * D,
            bytes_accessed=2 * count * depth * D + 6 * total * D,
            transcendentals=0,
        ),
        compiler_params=pltpu.CompilerParams(vmem_limit_bytes=48 * MIB),
        name="hidden",
    )(mask, *mine, *residual, *weights, layer_scale.reshape(1, D))


def norm_kernel(parts, part_ref, hidden_ref, *refs):
    stats_refs, (w_ref, b_ref), outs = refs[:SUBS], refs[SUBS : SUBS + 2], refs[SUBS + 2 :]
    total = hidden_ref.shape[0]
    rows, width = total // SUBS, D // parts
    means = [jnp.broadcast_to(ref[0:1, :], (128, total)).T for ref in stats_refs]
    spreads = [jnp.broadcast_to(ref[1:2, :], (128, total)).T for ref in stats_refs]
    for out in outs:
        if out.shape[1] > width:
            out[:, out.shape[1] - 128 :] = jnp.zeros((total, 128), BF16)
    for d in range(SUBS):
        where = [slice((d ^ e) * rows, ((d ^ e) + 1) * rows) for e in range(SUBS)]
        mean = sum(means[e][where[e], :] for e in range(SUBS)) / SUBS
        var = 0.0
        for e in range(SUBS):
            off = means[e][where[e], :] - mean
            var = var + spreads[e][where[e], :] + D * off * off
        inv = lax.rsqrt(var / (SUBS * D) + 1e-05)
        part = slice(d * rows, (d + 1) * rows)
        normed = (hidden_ref[part, :] - mean[:, 0:1]) * inv[:, 0:1] * w_ref[...] + b_ref[...]
        for i in range(parts):
            cut = normed[:, i * width : (i + 1) * width].astype(BF16)
            for e in range(parts):

                @pl.when((part_ref[0] ^ e) == i)
                def _():
                    outs[e][part, :width] = cut


def norm(hidden, stats, weight, bias, part, parts):
    total = hidden.shape[0]
    padded = pl.cdiv(D // parts, 128) * 128
    vmem = pl.BlockSpec(memory_space=pltpu.VMEM)
    return pl.pallas_call(
        functools.partial(norm_kernel, parts),
        in_specs=[pl.BlockSpec(memory_space=pltpu.SMEM)] + [vmem] * (SUBS + 3),
        out_specs=[vmem] * parts,
        out_shape=[jax.ShapeDtypeStruct((total, padded), BF16)] * parts,
        cost_estimate=pl.CostEstimate(
            flops=8 * total * D, bytes_accessed=6 * total * D, transcendentals=0
        ),
        compiler_params=pltpu.CompilerParams(vmem_limit_bytes=48 * MIB),
        name="norm",
    )(part.reshape(1), hidden, *stats, weight.reshape(1, D), bias.reshape(1, D))


def shares_kernel(parts, place_ref, owner_ref, *refs):
    slab_refs, w_ref, outs, ordered = refs[:parts], refs[parts], refs[parts + 1 : -1], refs[-1]
    merged, width = slab_refs[0].shape[0] // SUBS, w_ref.shape[0]
    half = merged // HALVES
    size = SUBS * half

    @pl.when(pl.program_id(0) == 0)
    def _():
        sub, part = place_ref[0], place_ref[1]
        for e in range(parts):
            for d in range(SUBS):
                target = owner_ref[(sub ^ d) * parts + (part ^ e)]
                f, g = lax.rem(target, parts) ^ part, lax.div(target, parts) ^ sub
                for h in range(HALVES):
                    start = pl.multiple_of((h * parts + f) * size + g * half, half)
                    low = d * merged + h * half
                    ordered[pl.ds(start, half), :] = slab_refs[e][low : low + half, :width]

    product = jnp.dot(ordered[...], w_ref[...], preferred_element_type=F32)
    for i, out in enumerate(outs):
        out[...] = product[i * size : (i + 1) * size, :].astype(BF16)


def shares_of(slab, place, owner, fc_weight):
    parts = len(slab)
    total = slab[0].shape[0]
    width, hid = fc_weight.shape
    block = 768
    size = total // HALVES
    outs = pl.pallas_call(
        functools.partial(shares_kernel, parts),
        grid=(hid // block,),
        in_specs=[pl.BlockSpec(memory_space=pltpu.SMEM)] * 2
        + [pl.BlockSpec(slab[0].shape, lambda n: (0, 0))] * parts
        + [pl.BlockSpec((width, block), lambda n: (0, n))],
        out_specs=[pl.BlockSpec((size, block), lambda n: (0, n))] * (HALVES * parts),
        out_shape=[jax.ShapeDtypeStruct((size, hid), BF16)] * (HALVES * parts),
        scratch_shapes=[pltpu.VMEM((parts * total, width), BF16)],
        cost_estimate=pl.CostEstimate(
            flops=2 * parts * total * width * hid,
            bytes_accessed=2 * width * hid + 2 * parts * total * (width + hid),
            transcendentals=0,
        ),
        compiler_params=pltpu.CompilerParams(vmem_limit_bytes=48 * MIB),
        name="shares",
    )(place, owner, *slab, fc_weight)
    return [outs[h * parts : (h + 1) * parts] for h in range(HALVES)]


def add_kernel(count, *refs):
    rows = refs[count].shape[0]
    for d in range(SUBS):
        part = slice(d * rows, (d + 1) * rows)
        total = refs[0][part, :].astype(F32)
        for ref in refs[1:count]:
            total += ref[part, :].astype(F32)
        refs[count + d][...] = total.astype(BF16)


def add(terms):
    rows, hid = terms[0].shape
    block = 1536
    return pl.pallas_call(
        functools.partial(add_kernel, len(terms)),
        grid=(hid // block,),
        in_specs=[pl.BlockSpec((rows, block), lambda n: (0, n))] * len(terms),
        out_specs=[pl.BlockSpec((rows // SUBS, block), lambda n: (0, n))] * SUBS,
        out_shape=[jax.ShapeDtypeStruct((rows // SUBS, hid), BF16)] * SUBS,
        cost_estimate=pl.CostEstimate(
            flops=len(terms) * rows * hid,
            bytes_accessed=2 * (len(terms) + 1) * rows * hid,
            transcendentals=0,
        ),
        compiler_params=pltpu.CompilerParams(vmem_limit_bytes=32 * MIB),
        name="add",
    )(*terms)


def per_device(
    residual_in,
    norm_gain,
    qkv_weight,
    qk_gain,
    out_weight,
    layer_scale,
    segment_ids,
    pad_mask,
    ln_weight,
    ln_bias,
    fc_weight,
    fc_bias,
    owner,
):
    x = residual_in[0]
    rows_here = x.shape[0]
    n_seq, n_rows = lax.axis_size("seq"), lax.axis_size("rows")
    row = lax.axis_index("rows")
    parts = n_rows // SUBS
    sub, part = lax.div(row, parts), lax.rem(row, parts)
    width = D // parts
    chunk = rows_here // CHUNKS
    merged = chunk // SUBS
    hid = fc_weight.shape[1]

    def over_seq(value, d):
        return lax.ppermute(value, "seq", [(i, i ^ d) for i in range(n_seq)])

    def over_sub(value, d):
        return lax.ppermute(value, "rows", [(i, i ^ (d * parts)) for i in range(n_rows)])

    def over_part(value, d):
        return lax.ppermute(value, "rows", [(i, i ^ d) for i in range(n_rows)])

    def pick(value, index, axis=0):
        return lax.dynamic_index_in_dim(value, index, axis, keepdims=False)

    fence = lax.optimization_barrier

    tokens = reorder(x, chunk)
    cuts = [0, rows_here // 4, rows_here * 3 // 4, rows_here]
    cut = [tokens[low:high] for low, high in zip(cuts, cuts[1:])]
    by_sub = tokens.reshape(CHUNKS, SUBS, merged, D)
    residual = {0: pick(by_sub, sub, 1)}
    to_send = {d: pick(by_sub, sub ^ d, 1) for d in range(1, SUBS)}
    share = out_weight.shape[0] // n_rows
    strip = lax.dynamic_slice_in_dim(out_weight, row * share, share, 0)
    group = max(1, min(n_seq, TILE // rows_here))
    projected, squares = {}, {}

    own_id = segment_ids[0, :1]
    leads = [own_id] + [over_seq(own_id, d) for d in range(group, n_seq, group)]
    strips = {d: over_seq(strip, d) for d in range(2, n_seq, 2)}
    far = {d: over_seq(cut[0], d) for d in range(2, n_seq, 2)}
    near = over_seq(tokens, 1)
    residual[1] = over_sub(to_send[1], 1)
    given, given_s = project([tokens, near], norm_gain, qkv_weight)
    for d in range(2):
        projected[d, 0], squares[d, 0] = given[d], given_s[d]
    state = leads, strips, far, residual, to_send, cut, squares, out_weight
    leads, strips, far, residual, to_send, cut, squares, out_weight = fence(state)
    leads = jnp.concatenate(leads)

    out_blocks = {0: out_weight}
    for d in range(2, n_seq, 2):
        out_blocks[d] = lax.all_gather(strips[d], "rows", axis=0, tiled=True)
    for i in range(len(cut)):
        coming = {}
        if i + 1 < len(cut):
            coming = {d: over_seq(cut[i + 1], d) for d in range(2, n_seq, 2)}
        if i == 0:
            residual[2] = over_sub(to_send[2], 2)
        if i == 1:
            residual[3] = over_sub(to_send[3][:1], 3)
            out_blocks[1] = over_seq(out_weight, 1)
        for d in range(2, n_seq, 2):
            far[d + 1] = over_seq(far[d], 1)
        given, given_s = project([far[d] for d in range(2, n_seq)], norm_gain, qkv_weight)
        for d in range(2, n_seq):
            projected[d, i], squares[d, i] = given[d - 2], given_s[d - 2]
        if i + 1 < len(cut):
            held = {d: residual[d] for d in range(3)}
            state = coming, held, to_send, cut, squares, out_weight
            far, held, to_send, cut, squares, out_weight = fence(state)
            residual.update(held)
    plan, pieces = [], []
    for d, i in sorted(projected):
        plan.append((d, cuts[i], projected[d, i].shape[0]))
        pieces.append(projected[d, i])

    here = jnp.concatenate([squares[key] for key in sorted(squares)], axis=1)
    here = jnp.transpose(here.reshape(2, n_seq, rows_here), (1, 0, 2))
    total = here
    for e in range(1, n_seq):
        there = over_seq(here, e)
        total = total + jnp.stack([there[d ^ e] for d in range(n_seq)])
    total = jnp.transpose(total, (1, 0, 2)).reshape(2, n_seq * rows_here)

    sub_ln = lax.dynamic_slice_in_dim(ln_weight, sub * D, D, 0)
    sub_bias = lax.dynamic_slice_in_dim(ln_bias, sub * D, D, 0)
    place = jnp.stack([sub, part])
    relative = np.array([d * parts + e for e in range(parts) for d in range(SUBS)], np.int32)

    def heads_of(j, sums):
        return attend(pieces, plan, rows_here, sums, leads, qk_gain, j * chunk, chunk)

    def gather_heads(heads):
        return [heads[0]] + [over_seq(heads[d], d) for d in range(1, n_seq)]

    def gather_rows(groups):
        packed = pack(groups, sub)
        return [packed[0]] + [over_sub(packed[d], d) for d in range(1, SUBS)]

    def to_hidden(j, mine):
        own = pad_mask[0, :1]
        return hidden_of(places[j], mine, residual, out_weights, layer_scale, own)

    def to_normed(hidden, stats):
        known = [stats] + [over_sub(stats, e) for e in range(1, SUBS)]
        return norm(hidden, known, sub_ln, sub_bias, part, parts), known

    def over_parts(values):
        return [values[0]] + [over_part(values[e], e) for e in range(1, parts)]

    def finish(terms, own_mask):
        pre = sum(term.astype(F32) for term in terms)
        return (jax.nn.gelu(pre + fc_bias, approximate=False) * own_mask).astype(BF16)

    heads_0 = heads_of(0, total)
    heads_0, total, out_blocks, residual = fence((heads_0, total, out_blocks, residual))
    places = [(0, 0, 0, 0), (1, 1, 1, 0)]
    residual = [residual[d] for d in range(SUBS)]

    for d in range(2, n_seq, 2):
        out_blocks[d + 1] = over_seq(out_blocks[d], 1)
    last = over_sub(to_send[3][1:], 3)
    heads_1 = heads_of(1, total)
    rows_0 = gather_rows(gather_heads(heads_0))
    heads_1, rows_0, out_blocks, last = fence((heads_1, rows_0, out_blocks, last))
    out_weights = [out_blocks[d] for d in range(n_seq)]

    hidden_0 = to_hidden(0, rows_0)
    groups_1 = gather_heads(heads_1)
    hidden_0, groups_1 = fence((hidden_0, groups_1))

    rows_1 = gather_rows(groups_1)
    normed_0, known = to_normed(*hidden_0)
    slab_0 = over_parts(normed_0)
    slab_0, known, rows_1 = fence((slab_0, known, rows_1))

    residual = [*residual[:3], last]
    normed_1, _ = to_normed(*to_hidden(1, rows_1))
    slab_0, known, normed_1 = fence((slab_0, known, normed_1))

    slab_1 = over_parts(normed_1)
    waiting = shares_of(slab_0, place, owner, fc_weight)
    slab_1, waiting, known = fence((slab_1, waiting, known))

    units = CHUNKS * HALVES
    by_part, by_sub, outs, own_mask = [], [], [], None
    for tick in range(units + 2):
        new_by_part, new_by_sub = [], []
        if waiting:
            new_by_part = [over_parts(waiting[0])]
            waiting = waiting[1:]
        if tick == 0:
            waiting = waiting + shares_of(slab_1, place, owner, fc_weight)
            line = jnp.stack([stats[2, 0] for stats in known])
            masks = jnp.concatenate(over_parts([line] * parts))
            given = (row ^ relative)[:, None] == jnp.arange(n_rows, dtype=jnp.int32)[None, :]
            given = given & (owner[None, :] == row)
            own_mask = jnp.sum(jnp.where(given, masks[:, None], 0.0))
        if by_part:
            summed = add(by_part[0])
            new_by_sub = [[summed[0]] + [over_sub(summed[d], d) for d in range(1, SUBS)]]
        if by_sub:
            outs = outs + [finish(by_sub[0], own_mask)]
        state = waiting, new_by_part, new_by_sub, outs, own_mask
        waiting, by_part, by_sub, outs, own_mask = fence(state)
    return jnp.concatenate(outs, axis=0)[None]


def solution(mesh):
    return jax.shard_map(
        per_device,
        mesh=mesh,
        in_specs=(
            P("rows", "seq", None),
            P(),
            P(None, "seq"),
            P(None, "seq"),
            P("seq", None),
            P(),
            P("rows", "seq"),
            P("rows", "seq"),
            P(),
            P(),
            P("rows", None),
            P(),
            P(),
        ),
        out_specs=P("rows", "seq", None),
        check_vma=False,
    )
```

```python
import functools
import math

import jax
import jax.numpy as jnp
import numpy as np
from jax import lax
from jax.experimental import pallas as pl
from jax.experimental.pallas import tpu as pltpu
from jax.sharding import PartitionSpec as P

D = 3200
HEAD_DIM = 128
HEADS = 16
GRID = 32
TILE = GRID * GRID
SUBS = 4
CHUNKS = 2
HALVES = 2
MIB = 1024 * 1024
BF16 = jnp.bfloat16
F32 = jnp.float32
TINY = pl.CostEstimate(flops=1, bytes_accessed=1, transcendentals=0)


def reorder_kernel(pick_ref, x_ref, out_ref):
    out_ref[...] = jnp.dot(pick_ref[...], x_ref[...], preferred_element_type=F32).astype(BF16)


def reorder(x, chunk):
    lines = chunk // (2 * GRID)
    source = np.arange(chunk).reshape(lines, 2, GRID // 2, 2).transpose(1, 3, 0, 2).reshape(chunk)
    pick = jnp.asarray(np.eye(chunk, dtype=np.float32)[source], BF16)
    return pl.pallas_call(
        reorder_kernel,
        grid=(x.shape[0] // chunk,),
        in_specs=[
            pl.BlockSpec((chunk, chunk), lambda i: (0, 0)),
            pl.BlockSpec((chunk, D), lambda i: (i, 0)),
        ],
        out_specs=pl.BlockSpec((chunk, D), lambda i: (i, 0)),
        out_shape=jax.ShapeDtypeStruct(x.shape, BF16),
        cost_estimate=pl.CostEstimate(
            flops=2 * x.shape[0] * chunk * D, bytes_accessed=4 * x.size, transcendentals=0
        ),
        compiler_params=pltpu.CompilerParams(vmem_limit_bytes=32 * MIB),
        name="reorder",
    )(pick, x)


def qkv_kernel(count, *refs):
    x_refs, gain_ref, w_ref = refs[:count], refs[count], refs[count + 1]
    out_refs = refs[count + 2 : 2 * count + 2]
    sq_refs = refs[2 * count + 2 : 3 * count + 2]
    normed, q_acc, k_acc = refs[3 * count + 2 :]
    head = pl.program_id(0)
    rows = x_refs[0].shape[0]
    step = 64

    @pl.when(head == 0)
    def _():
        for i in range(count):

            @pl.loop(0, rows // step)
            def _(b):
                part = pl.ds(pl.multiple_of(b * step, step), step)
                x = x_refs[i][part, :].astype(F32)
                inv = lax.rsqrt(jnp.mean(x * x, axis=-1, keepdims=True) + 1e-06)
                normed[i, part, :] = (x * inv * gain_ref[...]).astype(BF16)

        q_acc[...] = jnp.zeros_like(q_acc)
        k_acc[...] = jnp.zeros_like(k_acc)

    for i in range(count):
        product = jnp.dot(normed[i], w_ref[...], preferred_element_type=F32)
        out_refs[i][...] = product
        for first in range(0, product.shape[1], 3 * HEAD_DIM):
            q = product[:, first : first + HEAD_DIM]
            k = product[:, first + HEAD_DIM : first + 2 * HEAD_DIM]
            q_acc[i] += q * q
            k_acc[i] += k * k

    @pl.when(head == pl.num_programs(0) - 1)
    def _():
        for i in range(count):
            sq_refs[i][0:1, :] = jnp.sum(q_acc[i].T, axis=0, keepdims=True)
            sq_refs[i][1:2, :] = jnp.sum(k_acc[i].T, axis=0, keepdims=True)


def project(pieces, norm_gain, qkv_weight):
    count = len(pieces)
    rows = pieces[0].shape[0]
    width = qkv_weight.shape[1]
    heads = width // (3 * HEAD_DIM)
    block = 3 * HEAD_DIM * (2 if heads % 2 == 0 else 1)
    results = pl.pallas_call(
        functools.partial(qkv_kernel, count),
        grid=(width // block,),
        in_specs=[pl.BlockSpec((rows, D), lambda h: (0, 0))] * count
        + [
            pl.BlockSpec((1, D), lambda h: (0, 0)),
            pl.BlockSpec((D, block), lambda h: (0, h)),
        ],
        out_specs=[pl.BlockSpec((rows, block), lambda h: (0, h))] * count
        + [pl.BlockSpec((2, rows), lambda h: (0, 0))] * count,
        out_shape=[jax.ShapeDtypeStruct((rows, width), F32)] * count
        + [jax.ShapeDtypeStruct((2, rows), F32)] * count,
        scratch_shapes=[
            pltpu.VMEM((count, rows, D), BF16),
            pltpu.VMEM((count, rows, HEAD_DIM), F32),
            pltpu.VMEM((count, rows, HEAD_DIM), F32),
        ],
        cost_estimate=TINY,
        compiler_params=pltpu.CompilerParams(vmem_limit_bytes=56 * MIB),
        name="qkv",
    )(*pieces, norm_gain.reshape(1, D), qkv_weight)
    return results[:count], results[count:]


def attend_kernel(plan, rows, first, chunk, group, *refs):
    count = len(plan)
    blocks = plan[-1][0] + 1
    groups = blocks // group
    seg_refs, refs = refs[:groups], refs[groups:]
    sq_ref, gain_ref = refs[:2]
    p_refs = refs[2 : 2 + count]
    out_refs = refs[2 + count : 2 + count + blocks]
    q_scale, k_scale, q_all, k_all, v_all = refs[2 + count + blocks :]
    head = pl.program_id(0)
    factor = HEAD_DIM ** (-0.5) * math.log2(math.e)

    @pl.when(head == 0)
    def _():
        inv = lax.rsqrt(sq_ref[...] / (HEADS * HEAD_DIM) + 1e-06)
        for d in range(blocks):
            part = slice(d * rows, (d + 1) * rows)
            k_scale[part, :] = jnp.broadcast_to(inv[1:2, part], (HEAD_DIM, rows)).T
            q_wide = jnp.broadcast_to(inv[0:1, part] * factor, (HEAD_DIM, rows)).T
            q_scale[d * chunk : (d + 1) * chunk, :] = q_wide[first : first + chunk, :]
        v_all[:, HEAD_DIM:] = jnp.ones_like(v_all[:, HEAD_DIM:])

    for (d, start, size), p_ref in zip(plan, p_refs):
        part = slice(d * rows + start, d * rows + start + size)
        k = p_ref[:, HEAD_DIM : 2 * HEAD_DIM]
        k_all[part, :] = (k * k_scale[part, :] * gain_ref[1:2, :]).astype(BF16)
        v_all[part, :HEAD_DIM] = p_ref[:, 2 * HEAD_DIM :].astype(BF16)
        low, high = max(first, start), min(first + chunk, start + size)
        if low < high:
            part = slice(d * chunk + low - first, d * chunk + high - first)
            q = p_ref[low - start : high - start, :HEAD_DIM]
            q_all[part, :] = (q * q_scale[part, :] * gain_ref[0:1, :]).astype(BF16)

    keys = group * rows
    step = min(chunk, 128)

    def attend(d, begin, low, high):
        q = q_all[d * chunk + begin : d * chunk + begin + step, :]
        scores = lax.dot_general(
            q, k_all[low:high, :], (((1,), (1,)), ((), ())), preferred_element_type=F32
        )
        if groups > 2:
            own = d // group
            masked = []
            for g in range(groups):
                part = scores[:, g * keys : (g + 1) * keys]
                if g != own:
                    part = jnp.where(seg_refs[g][0] == seg_refs[own][0], part, -1e30)
                masked.append(part)
            scores = jnp.concatenate(masked, axis=1)
        peak = jnp.max(scores, axis=-1, keepdims=True)
        terms = jnp.exp2(scores - peak).astype(BF16)
        both = jnp.dot(terms, v_all[low:high, :], preferred_element_type=F32)
        out_refs[d][begin : begin + step, :] = (
            both[:, :HEAD_DIM] / both[:, HEAD_DIM:]
        ).astype(BF16)

    def attend_all(d, low, high):
        for begin in range(0, chunk, step):
            attend(d, begin, low, high)

    if groups != 2:
        for d in range(blocks):
            attend_all(d, 0, blocks * rows)
    else:
        joint = seg_refs[0][0] == seg_refs[1][0]

        @pl.when(joint)
        def _():
            for d in range(blocks):
                attend_all(d, 0, blocks * rows)

        @pl.when(jnp.logical_not(joint))
        def _():
            for d in range(blocks):
                own = d // group
                attend_all(d, own * keys, (own + 1) * keys)


def attend(pieces, plan, rows, squares, segments, qk_gain, first, chunk):
    blocks = plan[-1][0] + 1
    width = pieces[0].shape[1]
    heads = width // (3 * HEAD_DIM)
    total = blocks * rows
    group = max(1, min(blocks, TILE // rows))
    return pl.pallas_call(
        functools.partial(attend_kernel, plan, rows, first, chunk, group),
        grid=(heads,),
        in_specs=[pl.BlockSpec(memory_space=pltpu.SMEM)] * len(segments)
        + [
            pl.BlockSpec((2, total), lambda h: (0, 0)),
            pl.BlockSpec((2, HEAD_DIM), lambda h: (0, h)),
        ]
        + [pl.BlockSpec((size, 3 * HEAD_DIM), lambda h: (0, h)) for _, _, size in plan],
        out_specs=[pl.BlockSpec((chunk, HEAD_DIM), lambda h: (0, h))] * blocks,
        out_shape=[jax.ShapeDtypeStruct((chunk, heads * HEAD_DIM), BF16)] * blocks,
        scratch_shapes=[
            pltpu.VMEM((blocks * chunk, HEAD_DIM), F32),
            pltpu.VMEM((total, HEAD_DIM), F32),
            pltpu.VMEM((blocks * chunk, HEAD_DIM), BF16),
            pltpu.VMEM((total, HEAD_DIM), BF16),
            pltpu.VMEM((total, 2 * HEAD_DIM), BF16),
        ],
        cost_estimate=TINY,
        compiler_params=pltpu.CompilerParams(vmem_limit_bytes=56 * MIB),
        name="attend",
    )(*segments, squares, qk_gain, *pieces)


def pack_kernel(sub_ref, *refs):
    outs = refs[-SUBS:]
    rows, width = outs[0].shape[0], refs[0].shape[1]
    for d in range(SUBS):
        part = pl.ds(pl.multiple_of((sub_ref[0] ^ d) * rows, rows), rows)
        for i, ref in enumerate(refs[:-SUBS]):
            outs[d][:, i * width : (i + 1) * width] = ref[part, :]


def pack(groups, sub):
    chunk, width = groups[0].shape
    shape = (chunk // SUBS, width * len(groups))
    vmem = pl.BlockSpec(memory_space=pltpu.VMEM)
    return pl.pallas_call(
        pack_kernel,
        in_specs=[pl.BlockSpec(memory_space=pltpu.SMEM)] + [vmem] * len(groups),
        out_specs=[vmem] * SUBS,
        out_shape=[jax.ShapeDtypeStruct(shape, BF16)] * SUBS,
        compiler_params=pltpu.CompilerParams(vmem_limit_bytes=32 * MIB),
        name="pack",
    )(sub.reshape(1), *groups)


def hidden_kernel(sizes, strip_ref, mask_ref, *refs):
    count = sum(sizes)
    mine_refs, stream_refs = refs[:SUBS], refs[SUBS : 2 * SUBS]
    w_refs = refs[2 * SUBS : 2 * SUBS + count]
    scale_ref, hidden_ref, stats_ref, mine, mean_wide, spread_wide = refs[2 * SUBS + count :]
    rows = mine_refs[0].shape[0]
    depth, block = w_refs[0].shape
    n = pl.program_id(0)

    @pl.when(n == 0)
    def _():
        for i, size in enumerate(sizes):
            width = depth // size
            for k in range(size):
                start = i * depth + (strip_ref[0] ^ k) * width if size > 1 else i * depth
                columns = pl.ds(pl.multiple_of(start, width), width)
                low = i * depth + k * width
                for d in range(SUBS):
                    part = slice(d * rows, (d + 1) * rows)
                    mine[part, low : low + width] = mine_refs[d][:, columns]

    attn = None
    for i, size in enumerate(sizes):
        first = sum(sizes[:i])
        weight = [ref[...] for ref in w_refs[first : first + size]]
        weight = jnp.concatenate(weight, axis=0) if size > 1 else weight[0]
        product = jnp.dot(
            mine[:, i * depth : (i + 1) * depth], weight, preferred_element_type=F32
        )
        attn = product if attn is None else attn + product
    columns = pl.ds(pl.multiple_of(n * block, block), block)
    for d in range(SUBS):
        part = slice(d * rows, (d + 1) * rows)
        stream = stream_refs[d][0].astype(F32)
        hidden_ref[part, columns] = stream + scale_ref[...] * attn[part, :]

    @pl.when(n == pl.num_programs(0) - 1)
    def _():
        for d in range(SUBS):
            part = slice(d * rows, (d + 1) * rows)
            hidden = hidden_ref[part, :]
            mean = jnp.sum(hidden, axis=-1, keepdims=True) / D
            centre = hidden - mean
            spread = jnp.sum(centre * centre, axis=-1, keepdims=True)
            mean_wide[part, :] = jnp.broadcast_to(mean, (rows, 128))
            spread_wide[part, :] = jnp.broadcast_to(spread, (rows, 128))
        stats_ref[0:1, :] = mean_wide[...].T[0:1, :]
        stats_ref[1:2, :] = spread_wide[...].T[0:1, :]
        stats_ref[2:3, :] = jnp.full((1, SUBS * rows), mask_ref[0].astype(F32))


def hidden_of(places, mine, residual, weights, strip, layer_scale, mask):
    rows = mine[0].shape[0]
    count, depth, block = len(weights), weights[0][0].shape[0], 640
    sizes = [len(strips) for strips in weights]
    weights = [part for strips in weights for part in strips]
    total = SUBS * rows
    return pl.pallas_call(
        functools.partial(hidden_kernel, sizes),
        grid=(D // block,),
        in_specs=[pl.BlockSpec(memory_space=pltpu.SMEM)] * 2
        + [pl.BlockSpec(mine[0].shape, lambda n: (0, 0))] * SUBS
        + [pl.BlockSpec((1, rows, block), lambda n, j=j: (j, 0, n)) for j in places]
        + [pl.BlockSpec((part.shape[0], block), lambda n: (0, n)) for part in weights]
        + [pl.BlockSpec((1, block), lambda n: (0, n))],
        out_specs=[
            pl.BlockSpec((total, D), lambda n: (0, 0)),
            pl.BlockSpec((3, total), lambda n: (0, 0)),
        ],
        out_shape=[
            jax.ShapeDtypeStruct((total, D), F32),
            jax.ShapeDtypeStruct((3, total), F32),
        ],
        scratch_shapes=[
            pltpu.VMEM((total, count * depth), BF16),
            pltpu.VMEM((total, 128), F32),
            pltpu.VMEM((total, 128), F32),
        ],
        cost_estimate=pl.CostEstimate(
            flops=2 * total * count * depth * D,
            bytes_accessed=2 * count * depth * D + 6 * total * D,
            transcendentals=0,
        ),
        compiler_params=pltpu.CompilerParams(vmem_limit_bytes=48 * MIB),
        name="hidden",
    )(strip, mask, *mine, *residual, *weights, layer_scale.reshape(1, D))


def norm_kernel(parts, part_ref, hidden_ref, *refs):
    stats_refs, (w_ref, b_ref), outs = refs[:SUBS], refs[SUBS : SUBS + 2], refs[SUBS + 2 :]
    total = hidden_ref.shape[0]
    rows, width = total // SUBS, D // parts
    means = [jnp.broadcast_to(ref[0:1, :], (128, total)).T for ref in stats_refs]
    spreads = [jnp.broadcast_to(ref[1:2, :], (128, total)).T for ref in stats_refs]
    for out in outs:
        if out.shape[1] > width:
            out[:, out.shape[1] - 128 :] = jnp.zeros((total, 128), BF16)
    for d in range(SUBS):
        where = [slice((d ^ e) * rows, ((d ^ e) + 1) * rows) for e in range(SUBS)]
        mean = sum(means[e][where[e], :] for e in range(SUBS)) / SUBS
        var = 0.0
        for e in range(SUBS):
            off = means[e][where[e], :] - mean
            var = var + spreads[e][where[e], :] + D * off * off
        inv = lax.rsqrt(var / (SUBS * D) + 1e-05)
        part = slice(d * rows, (d + 1) * rows)
        normed = (hidden_ref[part, :] - mean[:, 0:1]) * inv[:, 0:1] * w_ref[...] + b_ref[...]
        for i in range(parts):
            cut = normed[:, i * width : (i + 1) * width].astype(BF16)
            for e in range(parts):

                @pl.when((part_ref[0] ^ e) == i)
                def _():
                    outs[e][part, :width] = cut


def norm(hidden, stats, weight, bias, part, parts):
    total = hidden.shape[0]
    padded = pl.cdiv(D // parts, 128) * 128
    vmem = pl.BlockSpec(memory_space=pltpu.VMEM)
    return pl.pallas_call(
        functools.partial(norm_kernel, parts),
        in_specs=[pl.BlockSpec(memory_space=pltpu.SMEM)] + [vmem] * (SUBS + 3),
        out_specs=[vmem] * parts,
        out_shape=[jax.ShapeDtypeStruct((total, padded), BF16)] * parts,
        cost_estimate=pl.CostEstimate(
            flops=8 * total * D, bytes_accessed=6 * total * D, transcendentals=0
        ),
        compiler_params=pltpu.CompilerParams(vmem_limit_bytes=48 * MIB),
        name="norm",
    )(part.reshape(1), hidden, *stats, weight.reshape(1, D), bias.reshape(1, D))


def shares_kernel(parts, place_ref, owner_ref, *refs):
    slab_refs, w_ref, outs, ordered = refs[:parts], refs[parts], refs[parts + 1 : -1], refs[-1]
    merged, width = slab_refs[0].shape[0] // SUBS, w_ref.shape[0]
    half = merged // HALVES
    size = SUBS * half

    @pl.when(pl.program_id(0) == 0)
    def _():
        sub, part = place_ref[0], place_ref[1]
        for e in range(parts):
            for d in range(SUBS):
                target = owner_ref[(sub ^ d) * parts + (part ^ e)]
                f, g = lax.rem(target, parts) ^ part, lax.div(target, parts) ^ sub
                for h in range(HALVES):
                    start = pl.multiple_of((h * parts + f) * size + g * half, half)
                    low = d * merged + h * half
                    ordered[pl.ds(start, half), :] = slab_refs[e][low : low + half, :width]

    product = jnp.dot(ordered[...], w_ref[...], preferred_element_type=F32)
    for i, out in enumerate(outs):
        out[...] = product[i * size : (i + 1) * size, :].astype(BF16)


def shares_of(slab, place, owner, fc_weight):
    parts = len(slab)
    total = slab[0].shape[0]
    width, hid = fc_weight.shape
    block = 1536
    size = total // HALVES
    outs = pl.pallas_call(
        functools.partial(shares_kernel, parts),
        grid=(hid // block,),
        in_specs=[pl.BlockSpec(memory_space=pltpu.SMEM)] * 2
        + [pl.BlockSpec(slab[0].shape, lambda n: (0, 0))] * parts
        + [pl.BlockSpec((width, block), lambda n: (0, n))],
        out_specs=[pl.BlockSpec((size, block), lambda n: (0, n))] * (HALVES * parts),
        out_shape=[jax.ShapeDtypeStruct((size, hid), BF16)] * (HALVES * parts),
        scratch_shapes=[pltpu.VMEM((parts * total, width), BF16)],
        cost_estimate=pl.CostEstimate(
            flops=2 * parts * total * width * hid,
            bytes_accessed=2 * width * hid + 2 * parts * total * (width + hid),
            transcendentals=0,
        ),
        compiler_params=pltpu.CompilerParams(vmem_limit_bytes=48 * MIB),
        name="shares",
    )(place, owner, *slab, fc_weight)
    return [outs[h * parts : (h + 1) * parts] for h in range(HALVES)]


def add_kernel(count, *refs):
    rows = refs[count].shape[0]
    for d in range(SUBS):
        part = slice(d * rows, (d + 1) * rows)
        total = refs[0][part, :].astype(F32)
        for ref in refs[1:count]:
            total += ref[part, :].astype(F32)
        refs[count + d][...] = total.astype(BF16)


def add(terms):
    rows, hid = terms[0].shape
    block = 1536
    return pl.pallas_call(
        functools.partial(add_kernel, len(terms)),
        grid=(hid // block,),
        in_specs=[pl.BlockSpec((rows, block), lambda n: (0, n))] * len(terms),
        out_specs=[pl.BlockSpec((rows // SUBS, block), lambda n: (0, n))] * SUBS,
        out_shape=[jax.ShapeDtypeStruct((rows // SUBS, hid), BF16)] * SUBS,
        cost_estimate=pl.CostEstimate(
            flops=len(terms) * rows * hid,
            bytes_accessed=2 * (len(terms) + 1) * rows * hid,
            transcendentals=0,
        ),
        compiler_params=pltpu.CompilerParams(vmem_limit_bytes=32 * MIB),
        name="add",
    )(*terms)


def per_device(
    residual_in,
    norm_gain,
    qkv_weight,
    qk_gain,
    out_weight,
    layer_scale,
    segment_ids,
    pad_mask,
    ln_weight,
    ln_bias,
    fc_weight,
    fc_bias,
    owner,
):
    x = residual_in[0]
    rows_here = x.shape[0]
    n_seq, n_rows = lax.axis_size("seq"), lax.axis_size("rows")
    row = lax.axis_index("rows")
    parts = n_rows // SUBS
    sub, part = lax.div(row, parts), lax.rem(row, parts)
    width = D // parts
    chunk = rows_here // CHUNKS
    merged = chunk // SUBS
    hid = fc_weight.shape[1]

    def over_seq(value, d):
        return lax.ppermute(value, "seq", [(i, i ^ d) for i in range(n_seq)])

    def over_sub(value, d):
        return lax.ppermute(value, "rows", [(i, i ^ (d * parts)) for i in range(n_rows)])

    def over_part(value, d):
        return lax.ppermute(value, "rows", [(i, i ^ d) for i in range(n_rows)])

    def pick(value, index, axis=0):
        return lax.dynamic_index_in_dim(value, index, axis, keepdims=False)

    fence = lax.optimization_barrier

    tokens = reorder(x, chunk)
    cuts = [0, rows_here // 4, rows_here * 3 // 4, rows_here]
    cut = [tokens[low:high] for low, high in zip(cuts, cuts[1:])]
    by_sub = tokens.reshape(CHUNKS, SUBS, merged, D)
    residual = {0: pick(by_sub, sub, 1)}
    to_send = {d: pick(by_sub, sub ^ d, 1) for d in range(1, SUBS)}
    depth = out_weight.shape[0]
    across = max(1, min(2, depth // 256, parts))
    strip = lax.bitwise_and(part, across - 1) * 2 + lax.bitwise_and(sub, 1)
    size = depth // (2 * across)
    own_strip = lax.dynamic_slice_in_dim(out_weight, strip * size, size, 0)
    group = max(1, min(n_seq, TILE // rows_here))
    projected, squares = {}, {}

    own_id = segment_ids[0, :1]
    leads = [own_id] + [over_seq(own_id, d) for d in range(group, n_seq, group)]
    strips = {(d, 0): over_seq(own_strip, d) for d in range(2, n_seq, 2)}
    far = {d: over_seq(cut[0], d) for d in range(2, n_seq, 2)}
    near = over_seq(tokens, 1)
    residual[1] = over_sub(to_send[1], 1)
    residual[2] = over_sub(to_send[2][:1], 2)
    given, given_s = project([tokens, near], norm_gain, qkv_weight)
    for d in range(2):
        projected[d, 0], squares[d, 0] = given[d], given_s[d]
    state = leads, strips, far, residual, to_send, cut, squares, out_weight
    leads, strips, far, residual, to_send, cut, squares, out_weight = fence(state)

    for i in range(len(cut)):
        coming = {}
        if i + 1 < len(cut):
            coming = {d: over_seq(cut[i + 1], d) for d in range(2, n_seq, 2)}
        arrived = dict(strips)
        for d, k in [key for key in arrived if key[0] % 2 == 0]:
            if k == 0 and i == 0:
                strips[d, 1] = over_sub(arrived[d, 0], 1)
            if k == i and across == 2:
                strips[d, 2 + k] = over_part(arrived[d, k], 1)
            if (d + 1, k) not in strips:
                strips[d + 1, k] = over_seq(arrived[d, k], 1)
        if i == 0:
            residual[3] = over_sub(to_send[3][:1], 3)
        if i == 1:
            last = {2: over_sub(to_send[2][1:], 2)}
            out_near = over_seq(out_weight, 1)
        for d in range(2, n_seq, 2):
            far[d + 1] = over_seq(far[d], 1)
        given, given_s = project([far[d] for d in range(2, n_seq)], norm_gain, qkv_weight)
        for d in range(2, n_seq):
            projected[d, i], squares[d, i] = given[d - 2], given_s[d - 2]
        if i + 1 < len(cut):
            held = last if i == 1 else {}
            state = coming, residual, to_send, cut, squares, out_weight, strips, held
            far, residual, to_send, cut, squares, out_weight, strips, last = fence(state)
    plan, pieces = [], []
    for d, i in sorted(projected):
        plan.append((d, cuts[i], projected[d, i].shape[0]))
        pieces.append(projected[d, i])

    here = jnp.concatenate([squares[key] for key in sorted(squares)], axis=1)
    here = jnp.transpose(here.reshape(2, n_seq, rows_here), (1, 0, 2))
    total = here
    for e in range(1, n_seq):
        there = over_seq(here, e)
        total = total + jnp.stack([there[d ^ e] for d in range(n_seq)])
    total = jnp.transpose(total, (1, 0, 2)).reshape(2, n_seq * rows_here)

    sub_ln = lax.dynamic_slice_in_dim(ln_weight, sub * D, D, 0)
    sub_bias = lax.dynamic_slice_in_dim(ln_bias, sub * D, D, 0)
    place = jnp.stack([sub, part])
    relative = np.array([d * parts + e for e in range(parts) for d in range(SUBS)], np.int32)

    places = [(0, 0, 0, 0), (1, 1, 0, 0)]

    def heads_of(j, sums):
        return attend(pieces, plan, rows_here, sums, leads, qk_gain, j * chunk, chunk)

    def gather_heads(heads):
        return [heads[0]] + [over_seq(heads[d], d) for d in range(1, n_seq)]

    def gather_rows(packed):
        return [packed[0]] + [over_sub(packed[d], d) for d in range(1, SUBS)]

    def to_hidden(j, mine):
        own = pad_mask[0, :1]
        return hidden_of(
            places[j], mine, residual, out_weights, strip.reshape(1), layer_scale, own
        )

    def to_normed(hidden, stats):
        known = [stats] + [over_sub(stats, e) for e in range(1, SUBS)]
        return norm(hidden, known, sub_ln, sub_bias, part, parts), known

    def over_parts(values):
        return [values[0]] + [over_part(values[e], e) for e in range(1, parts)]

    def finish(terms, own_mask):
        pre = sum(term.astype(F32) for term in terms)
        return (jax.nn.gelu(pre + fc_bias, approximate=False) * own_mask).astype(BF16)

    total, to_send, last, strips = fence((total, to_send, last, strips))

    last[3] = over_sub(to_send[3][1:], 3)
    heads_0 = heads_of(0, total)
    heads_0, total, last = fence((heads_0, total, last))

    heads_1 = heads_of(1, total)
    groups_0 = gather_heads(heads_0)
    heads_1, groups_0 = fence((heads_1, groups_0))

    rows_0 = gather_rows(pack(groups_0, sub))
    packed_1 = pack(gather_heads(heads_1), sub)
    rows_0, packed_1 = fence((rows_0, packed_1))

    out_weights = [[out_weight], [out_near]]
    for d in range(2, n_seq):
        out_weights.append([strips[d, k] for k in range(2 * across)])
    residual = [residual[d] for d in range(SUBS)]
    rows_1 = gather_rows(packed_1)
    hidden_0 = to_hidden(0, rows_0)
    hidden_0, rows_1 = fence((hidden_0, rows_1))

    normed_0, known = to_normed(*hidden_0)
    normed_0, known, rows_1 = fence((normed_0, known, rows_1))

    slab_0 = over_parts(normed_0)
    residual = [*residual[:2], last[2], last[3]]
    normed_1, _ = to_normed(*to_hidden(1, rows_1))
    slab_0, known, normed_1 = fence((slab_0, known, normed_1))

    slab_1 = over_parts(normed_1)
    waiting = shares_of(slab_0, place, owner, fc_weight)
    slab_1, waiting, known = fence((slab_1, waiting, known))

    units = CHUNKS * HALVES
    by_part, by_sub, outs, own_mask = [], [], [], None
    for tick in range(units + 2):
        new_by_part, new_by_sub = [], []
        if waiting:
            new_by_part = [over_parts(waiting[0])]
            waiting = waiting[1:]
        if tick == 0:
            waiting = waiting + shares_of(slab_1, place, owner, fc_weight)
        if tick == 1:
            line = jnp.stack([stats[2, 0] for stats in known])
            own_mask = over_parts([line] * parts)
        if tick == 2:
            masks = jnp.concatenate(own_mask)
            given = (row ^ relative)[:, None] == jnp.arange(n_rows, dtype=jnp.int32)[None, :]
            given = given & (owner[None, :] == row)
            own_mask = jnp.sum(jnp.where(given, masks[:, None], 0.0))
        if by_part:
            summed = add(by_part[0])
            new_by_sub = [[summed[0]] + [over_sub(summed[d], d) for d in range(1, SUBS)]]
        if by_sub:
            outs = outs + [finish(by_sub[0], own_mask)]
        state = waiting, new_by_part, new_by_sub, outs, own_mask, known
        waiting, by_part, by_sub, outs, own_mask, known = fence(state)
    return jnp.concatenate(outs, axis=0)[None]


def solution(mesh):
    return jax.shard_map(
        per_device,
        mesh=mesh,
        in_specs=(
            P("rows", "seq", None),
            P(),
            P(None, "seq"),
            P(None, "seq"),
            P("seq", None),
            P(),
            P("rows", "seq"),
            P("rows", "seq"),
            P(),
            P(),
            P("rows", None),
            P(),
            P(),
        ),
        out_specs=P("rows", "seq", None),
        check_vma=False,
    )
```

```python
import functools
import math

import jax
import jax.numpy as jnp
import numpy as np
from jax import lax
from jax.experimental import pallas as pl
from jax.experimental.pallas import tpu as pltpu
from jax.sharding import PartitionSpec as P

D = 3200
HEAD_DIM = 128
HEADS = 16
GRID = 32
TILE = GRID * GRID
SUBS = 4
CHUNKS = 2
HALVES = 2
MIB = 1024 * 1024
BF16 = jnp.bfloat16
F32 = jnp.float32
TINY = pl.CostEstimate(flops=1, bytes_accessed=1, transcendentals=0)


def reorder_kernel(pick_ref, x_ref, out_ref):
    out_ref[...] = jnp.dot(pick_ref[...], x_ref[...], preferred_element_type=F32).astype(BF16)


def reorder(x, chunk):
    lines = chunk // (2 * GRID)
    source = np.arange(chunk).reshape(lines, 2, GRID // 2, 2).transpose(1, 3, 0, 2).reshape(chunk)
    pick = jnp.asarray(np.eye(chunk, dtype=np.float32)[source], BF16)
    return pl.pallas_call(
        reorder_kernel,
        grid=(x.shape[0] // chunk,),
        in_specs=[
            pl.BlockSpec((chunk, chunk), lambda i: (0, 0)),
            pl.BlockSpec((chunk, D), lambda i: (i, 0)),
        ],
        out_specs=pl.BlockSpec((chunk, D), lambda i: (i, 0)),
        out_shape=jax.ShapeDtypeStruct(x.shape, BF16),
        cost_estimate=pl.CostEstimate(
            flops=2 * x.shape[0] * chunk * D, bytes_accessed=4 * x.size, transcendentals=0
        ),
        compiler_params=pltpu.CompilerParams(vmem_limit_bytes=32 * MIB),
        name="reorder",
    )(pick, x)


def qkv_kernel(count, *refs):
    x_refs, gain_ref, w_ref = refs[:count], refs[count], refs[count + 1]
    out_refs = refs[count + 2 : 2 * count + 2]
    sq_refs = refs[2 * count + 2 : 3 * count + 2]
    normed, q_acc, k_acc = refs[3 * count + 2 :]
    head = pl.program_id(0)
    rows = x_refs[0].shape[0]
    step = 64

    @pl.when(head == 0)
    def _():
        for i in range(count):

            @pl.loop(0, rows // step)
            def _(b):
                part = pl.ds(pl.multiple_of(b * step, step), step)
                x = x_refs[i][part, :].astype(F32)
                inv = lax.rsqrt(jnp.mean(x * x, axis=-1, keepdims=True) + 1e-06)
                normed[i, part, :] = (x * inv * gain_ref[...]).astype(BF16)

        q_acc[...] = jnp.zeros_like(q_acc)
        k_acc[...] = jnp.zeros_like(k_acc)

    for i in range(count):
        product = jnp.dot(normed[i], w_ref[...], preferred_element_type=F32)
        out_refs[i][...] = product
        for first in range(0, product.shape[1], 3 * HEAD_DIM):
            q = product[:, first : first + HEAD_DIM]
            k = product[:, first + HEAD_DIM : first + 2 * HEAD_DIM]
            q_acc[i] += q * q
            k_acc[i] += k * k

    @pl.when(head == pl.num_programs(0) - 1)
    def _():
        for i in range(count):
            sq_refs[i][0:1, :] = jnp.sum(q_acc[i].T, axis=0, keepdims=True)
            sq_refs[i][1:2, :] = jnp.sum(k_acc[i].T, axis=0, keepdims=True)


def project(pieces, norm_gain, qkv_weight):
    count = len(pieces)
    rows = pieces[0].shape[0]
    width = qkv_weight.shape[1]
    heads = width // (3 * HEAD_DIM)
    block = 3 * HEAD_DIM * (2 if heads % 2 == 0 else 1)
    results = pl.pallas_call(
        functools.partial(qkv_kernel, count),
        grid=(width // block,),
        in_specs=[pl.BlockSpec((rows, D), lambda h: (0, 0))] * count
        + [
            pl.BlockSpec((1, D), lambda h: (0, 0)),
            pl.BlockSpec((D, block), lambda h: (0, h)),
        ],
        out_specs=[pl.BlockSpec((rows, block), lambda h: (0, h))] * count
        + [pl.BlockSpec((2, rows), lambda h: (0, 0))] * count,
        out_shape=[jax.ShapeDtypeStruct((rows, width), F32)] * count
        + [jax.ShapeDtypeStruct((2, rows), F32)] * count,
        scratch_shapes=[
            pltpu.VMEM((count, rows, D), BF16),
            pltpu.VMEM((count, rows, HEAD_DIM), F32),
            pltpu.VMEM((count, rows, HEAD_DIM), F32),
        ],
        cost_estimate=TINY,
        compiler_params=pltpu.CompilerParams(vmem_limit_bytes=56 * MIB),
        name="qkv",
    )(*pieces, norm_gain.reshape(1, D), qkv_weight)
    return results[:count], results[count:]


def attend_kernel(plan, rows, first, chunk, group, *refs):
    count = len(plan)
    blocks = plan[-1][0] + 1
    groups = blocks // group
    seg_refs, refs = refs[:groups], refs[groups:]
    sq_ref, gain_ref = refs[:2]
    p_refs = refs[2 : 2 + count]
    out_refs = refs[2 + count : 2 + count + blocks]
    q_scale, k_scale, q_all, k_all, v_all = refs[2 + count + blocks :]
    head = pl.program_id(0)
    factor = HEAD_DIM ** (-0.5) * math.log2(math.e)

    @pl.when(head == 0)
    def _():
        inv = lax.rsqrt(sq_ref[...] / (HEADS * HEAD_DIM) + 1e-06)
        for d in range(blocks):
            part = slice(d * rows, (d + 1) * rows)
            k_scale[part, :] = jnp.broadcast_to(inv[1:2, part], (HEAD_DIM, rows)).T
            q_wide = jnp.broadcast_to(inv[0:1, part] * factor, (HEAD_DIM, rows)).T
            q_scale[d * chunk : (d + 1) * chunk, :] = q_wide[first : first + chunk, :]
        v_all[:, HEAD_DIM:] = jnp.ones_like(v_all[:, HEAD_DIM:])

    for (d, start, size), p_ref in zip(plan, p_refs):
        part = slice(d * rows + start, d * rows + start + size)
        k = p_ref[:, HEAD_DIM : 2 * HEAD_DIM]
        k_all[part, :] = (k * k_scale[part, :] * gain_ref[1:2, :]).astype(BF16)
        v_all[part, :HEAD_DIM] = p_ref[:, 2 * HEAD_DIM :].astype(BF16)
        low, high = max(first, start), min(first + chunk, start + size)
        if low < high:
            part = slice(d * chunk + low - first, d * chunk + high - first)
            q = p_ref[low - start : high - start, :HEAD_DIM]
            q_all[part, :] = (q * q_scale[part, :] * gain_ref[0:1, :]).astype(BF16)

    keys = group * rows
    step = min(chunk, 128)

    def attend(d, begin, low, high):
        q = q_all[d * chunk + begin : d * chunk + begin + step, :]
        scores = lax.dot_general(
            q, k_all[low:high, :], (((1,), (1,)), ((), ())), preferred_element_type=F32
        )
        if groups > 2:
            own = d // group
            masked = []
            for g in range(groups):
                part = scores[:, g * keys : (g + 1) * keys]
                if g != own:
                    part = jnp.where(seg_refs[g][0] == seg_refs[own][0], part, -1e30)
                masked.append(part)
            scores = jnp.concatenate(masked, axis=1)
        peak = jnp.max(scores, axis=-1, keepdims=True)
        terms = jnp.exp2(scores - peak).astype(BF16)
        both = jnp.dot(terms, v_all[low:high, :], preferred_element_type=F32)
        out_refs[d][begin : begin + step, :] = (
            both[:, :HEAD_DIM] / both[:, HEAD_DIM:]
        ).astype(BF16)

    def attend_all(d, low, high):
        for begin in range(0, chunk, step):
            attend(d, begin, low, high)

    if groups != 2:
        for d in range(blocks):
            attend_all(d, 0, blocks * rows)
    else:
        joint = seg_refs[0][0] == seg_refs[1][0]

        @pl.when(joint)
        def _():
            for d in range(blocks):
                attend_all(d, 0, blocks * rows)

        @pl.when(jnp.logical_not(joint))
        def _():
            for d in range(blocks):
                own = d // group
                attend_all(d, own * keys, (own + 1) * keys)


def attend(pieces, plan, rows, squares, segments, qk_gain, first, chunk):
    blocks = plan[-1][0] + 1
    width = pieces[0].shape[1]
    heads = width // (3 * HEAD_DIM)
    total = blocks * rows
    group = max(1, min(blocks, TILE // rows))
    return pl.pallas_call(
        functools.partial(attend_kernel, plan, rows, first, chunk, group),
        grid=(heads,),
        in_specs=[pl.BlockSpec(memory_space=pltpu.SMEM)] * len(segments)
        + [
            pl.BlockSpec((2, total), lambda h: (0, 0)),
            pl.BlockSpec((2, HEAD_DIM), lambda h: (0, h)),
        ]
        + [pl.BlockSpec((size, 3 * HEAD_DIM), lambda h: (0, h)) for _, _, size in plan],
        out_specs=[pl.BlockSpec((chunk, HEAD_DIM), lambda h: (0, h))] * blocks,
        out_shape=[jax.ShapeDtypeStruct((chunk, heads * HEAD_DIM), BF16)] * blocks,
        scratch_shapes=[
            pltpu.VMEM((blocks * chunk, HEAD_DIM), F32),
            pltpu.VMEM((total, HEAD_DIM), F32),
            pltpu.VMEM((blocks * chunk, HEAD_DIM), BF16),
            pltpu.VMEM((total, HEAD_DIM), BF16),
            pltpu.VMEM((total, 2 * HEAD_DIM), BF16),
        ],
        cost_estimate=TINY,
        compiler_params=pltpu.CompilerParams(vmem_limit_bytes=56 * MIB),
        name="attend",
    )(*segments, squares, qk_gain, *pieces)


def pack_kernel(sub_ref, *refs):
    outs = refs[-SUBS:]
    rows, width = outs[0].shape[0], refs[0].shape[1]
    for d in range(SUBS):
        part = pl.ds(pl.multiple_of((sub_ref[0] ^ d) * rows, rows), rows)
        for i, ref in enumerate(refs[:-SUBS]):
            outs[d][:, i * width : (i + 1) * width] = ref[part, :]


def pack(groups, sub):
    chunk, width = groups[0].shape
    shape = (chunk // SUBS, width * len(groups))
    vmem = pl.BlockSpec(memory_space=pltpu.VMEM)
    return pl.pallas_call(
        pack_kernel,
        in_specs=[pl.BlockSpec(memory_space=pltpu.SMEM)] + [vmem] * len(groups),
        out_specs=[vmem] * SUBS,
        out_shape=[jax.ShapeDtypeStruct(shape, BF16)] * SUBS,
        compiler_params=pltpu.CompilerParams(vmem_limit_bytes=32 * MIB),
        name="pack",
    )(sub.reshape(1), *groups)


def hidden_kernel(sizes, strip_ref, mask_ref, *refs):
    count = sum(sizes)
    mine_refs, stream_refs = refs[:SUBS], refs[SUBS : 2 * SUBS]
    w_refs = refs[2 * SUBS : 2 * SUBS + count]
    scale_ref, hidden_ref, stats_ref, mine, mean_wide, spread_wide = refs[2 * SUBS + count :]
    rows = mine_refs[0].shape[0]
    depth, block = w_refs[0].shape
    n = pl.program_id(0)

    @pl.when(n == 0)
    def _():
        for i, size in enumerate(sizes):
            width = depth // size
            for k in range(size):
                start = i * depth + (strip_ref[0] ^ k) * width if size > 1 else i * depth
                columns = pl.ds(pl.multiple_of(start, width), width)
                low = i * depth + k * width
                for d in range(SUBS):
                    part = slice(d * rows, (d + 1) * rows)
                    mine[part, low : low + width] = mine_refs[d][:, columns]

    attn = None
    for i, size in enumerate(sizes):
        first = sum(sizes[:i])
        weight = [ref[...] for ref in w_refs[first : first + size]]
        weight = jnp.concatenate(weight, axis=0) if size > 1 else weight[0]
        product = jnp.dot(
            mine[:, i * depth : (i + 1) * depth], weight, preferred_element_type=F32
        )
        attn = product if attn is None else attn + product
    columns = pl.ds(pl.multiple_of(n * block, block), block)
    for d in range(SUBS):
        part = slice(d * rows, (d + 1) * rows)
        stream = stream_refs[d][0].astype(F32)
        hidden_ref[part, columns] = stream + scale_ref[...] * attn[part, :]

    @pl.when(n == pl.num_programs(0) - 1)
    def _():
        for d in range(SUBS):
            part = slice(d * rows, (d + 1) * rows)
            hidden = hidden_ref[part, :]
            mean = jnp.sum(hidden, axis=-1, keepdims=True) / D
            centre = hidden - mean
            spread = jnp.sum(centre * centre, axis=-1, keepdims=True)
            mean_wide[part, :] = jnp.broadcast_to(mean, (rows, 128))
            spread_wide[part, :] = jnp.broadcast_to(spread, (rows, 128))
        stats_ref[0:1, :] = mean_wide[...].T[0:1, :]
        stats_ref[1:2, :] = spread_wide[...].T[0:1, :]
        stats_ref[2:3, :] = jnp.full((1, SUBS * rows), mask_ref[0].astype(F32))


def hidden_of(places, mine, residual, weights, strip, layer_scale, mask):
    rows = mine[0].shape[0]
    count, depth, block = len(weights), weights[0][0].shape[0], D
    sizes = [len(strips) for strips in weights]
    weights = [part for strips in weights for part in strips]
    total = SUBS * rows
    return pl.pallas_call(
        functools.partial(hidden_kernel, sizes),
        grid=(D // block,),
        in_specs=[pl.BlockSpec(memory_space=pltpu.SMEM)] * 2
        + [pl.BlockSpec(mine[0].shape, lambda n: (0, 0))] * SUBS
        + [pl.BlockSpec((1, rows, block), lambda n, j=j: (j, 0, n)) for j in places]
        + [pl.BlockSpec((part.shape[0], block), lambda n: (0, n)) for part in weights]
        + [pl.BlockSpec((1, block), lambda n: (0, n))],
        out_specs=[
            pl.BlockSpec((total, D), lambda n: (0, 0)),
            pl.BlockSpec((3, total), lambda n: (0, 0)),
        ],
        out_shape=[
            jax.ShapeDtypeStruct((total, D), F32),
            jax.ShapeDtypeStruct((3, total), F32),
        ],
        scratch_shapes=[
            pltpu.VMEM((total, count * depth), BF16),
            pltpu.VMEM((total, 128), F32),
            pltpu.VMEM((total, 128), F32),
        ],
        cost_estimate=pl.CostEstimate(
            flops=2 * total * count * depth * D,
            bytes_accessed=2 * count * depth * D + 6 * total * D,
            transcendentals=0,
        ),
        compiler_params=pltpu.CompilerParams(vmem_limit_bytes=48 * MIB),
        name="hidden",
    )(strip, mask, *mine, *residual, *weights, layer_scale.reshape(1, D))


def norm_kernel(parts, part_ref, hidden_ref, *refs):
    stats_refs, (w_ref, b_ref) = refs[:SUBS], refs[SUBS : SUBS + 2]
    outs, line_ref = refs[SUBS + 2 : -1], refs[-1]
    total = hidden_ref.shape[0]
    rows, width = total // SUBS, D // parts
    for e in range(SUBS):
        line_ref[e : e + 1, :] = stats_refs[e][2:3, :128]
    means = [jnp.broadcast_to(ref[0:1, :], (128, total)).T for ref in stats_refs]
    spreads = [jnp.broadcast_to(ref[1:2, :], (128, total)).T for ref in stats_refs]
    for out in outs:
        if out.shape[1] > width:
            out[:, out.shape[1] - 128 :] = jnp.zeros((total, 128), BF16)
    for d in range(SUBS):
        where = [slice((d ^ e) * rows, ((d ^ e) + 1) * rows) for e in range(SUBS)]
        mean = sum(means[e][where[e], :] for e in range(SUBS)) / SUBS
        var = 0.0
        for e in range(SUBS):
            off = means[e][where[e], :] - mean
            var = var + spreads[e][where[e], :] + D * off * off
        inv = lax.rsqrt(var / (SUBS * D) + 1e-05)
        part = slice(d * rows, (d + 1) * rows)
        normed = (hidden_ref[part, :] - mean[:, 0:1]) * inv[:, 0:1] * w_ref[...] + b_ref[...]
        for i in range(parts):
            cut = normed[:, i * width : (i + 1) * width].astype(BF16)
            for e in range(parts):

                @pl.when((part_ref[0] ^ e) == i)
                def _():
                    outs[e][part, :width] = cut


def norm(hidden, stats, weight, bias, part, parts):
    total = hidden.shape[0]
    padded = pl.cdiv(D // parts, 128) * 128
    vmem = pl.BlockSpec(memory_space=pltpu.VMEM)
    return pl.pallas_call(
        functools.partial(norm_kernel, parts),
        in_specs=[pl.BlockSpec(memory_space=pltpu.SMEM)] + [vmem] * (SUBS + 3),
        out_specs=[vmem] * (parts + 1),
        out_shape=[jax.ShapeDtypeStruct((total, padded), BF16)] * parts
        + [jax.ShapeDtypeStruct((SUBS, 128), F32)],
        cost_estimate=TINY,
        compiler_params=pltpu.CompilerParams(vmem_limit_bytes=48 * MIB),
        name="norm",
    )(part.reshape(1), hidden, *stats, weight.reshape(1, D), bias.reshape(1, D))


def shares_kernel(parts, place_ref, owner_ref, *refs):
    slab_refs, w_ref, outs, ordered = refs[:parts], refs[parts], refs[parts + 1 : -1], refs[-1]
    merged, width = slab_refs[0].shape[0] // SUBS, w_ref.shape[0]
    half = merged // HALVES
    size = SUBS * half

    @pl.when(pl.program_id(0) == 0)
    def _():
        sub, part = place_ref[0], place_ref[1]
        for e in range(parts):
            for d in range(SUBS):
                target = owner_ref[(sub ^ d) * parts + (part ^ e)]
                f, g = lax.rem(target, parts) ^ part, lax.div(target, parts) ^ sub
                for h in range(HALVES):
                    start = pl.multiple_of((h * parts + f) * size + g * half, half)
                    low = d * merged + h * half
                    ordered[pl.ds(start, half), :] = slab_refs[e][low : low + half, :width]

    product = jnp.dot(ordered[...], w_ref[...], preferred_element_type=F32)
    for i, out in enumerate(outs):
        out[...] = product[i * size : (i + 1) * size, :].astype(BF16)


def shares_of(slab, place, owner, fc_weight):
    parts = len(slab)
    total = slab[0].shape[0]
    width, hid = fc_weight.shape
    block = 1536
    size = total // HALVES
    outs = pl.pallas_call(
        functools.partial(shares_kernel, parts),
        grid=(hid // block,),
        in_specs=[pl.BlockSpec(memory_space=pltpu.SMEM)] * 2
        + [pl.BlockSpec(slab[0].shape, lambda n: (0, 0))] * parts
        + [pl.BlockSpec((width, block), lambda n: (0, n))],
        out_specs=[pl.BlockSpec((size, block), lambda n: (0, n))] * (HALVES * parts),
        out_shape=[jax.ShapeDtypeStruct((size, hid), BF16)] * (HALVES * parts),
        scratch_shapes=[pltpu.VMEM((parts * total, width), BF16)],
        cost_estimate=pl.CostEstimate(
            flops=2 * parts * total * width * hid,
            bytes_accessed=2 * width * hid + 2 * parts * total * (width + hid),
            transcendentals=0,
        ),
        compiler_params=pltpu.CompilerParams(vmem_limit_bytes=48 * MIB),
        name="shares",
    )(place, owner, *slab, fc_weight)
    return [outs[h * parts : (h + 1) * parts] for h in range(HALVES)]


def add_kernel(count, *refs):
    rows = refs[count].shape[0]
    for d in range(SUBS):
        part = slice(d * rows, (d + 1) * rows)
        total = refs[0][part, :].astype(F32)
        for ref in refs[1:count]:
            total += ref[part, :].astype(F32)
        refs[count + d][...] = total.astype(BF16)


def add(terms):
    rows, hid = terms[0].shape
    block = 1536
    return pl.pallas_call(
        functools.partial(add_kernel, len(terms)),
        grid=(hid // block,),
        in_specs=[pl.BlockSpec((rows, block), lambda n: (0, n))] * len(terms),
        out_specs=[pl.BlockSpec((rows // SUBS, block), lambda n: (0, n))] * SUBS,
        out_shape=[jax.ShapeDtypeStruct((rows // SUBS, hid), BF16)] * SUBS,
        cost_estimate=pl.CostEstimate(
            flops=len(terms) * rows * hid,
            bytes_accessed=2 * (len(terms) + 1) * rows * hid,
            transcendentals=0,
        ),
        compiler_params=pltpu.CompilerParams(vmem_limit_bytes=32 * MIB),
        name="add",
    )(*terms)


def finish_kernel(mask_ref, bias_ref, *refs):
    pre = refs[0][...].astype(F32)
    for ref in refs[1:-1]:
        pre += ref[...].astype(F32)
    pre += bias_ref[...]
    half = 0.5 * pre * (1.0 + lax.erf(pre * math.sqrt(0.5)))
    refs[-1][...] = (half * mask_ref[0]).astype(BF16)


def finish(terms, bias, mask):
    rows, hid = terms[0].shape
    block = 1536
    return pl.pallas_call(
        finish_kernel,
        grid=(hid // block,),
        in_specs=[
            pl.BlockSpec(memory_space=pltpu.SMEM),
            pl.BlockSpec((1, block), lambda n: (0, n)),
        ]
        + [pl.BlockSpec((rows, block), lambda n: (0, n))] * len(terms),
        out_specs=pl.BlockSpec((rows, block), lambda n: (0, n)),
        out_shape=jax.ShapeDtypeStruct((rows, hid), BF16),
        cost_estimate=TINY,
        compiler_params=pltpu.CompilerParams(vmem_limit_bytes=32 * MIB),
        name="finish",
    )(mask, bias.reshape(1, hid), *terms)


def per_device(
    residual_in,
    norm_gain,
    qkv_weight,
    qk_gain,
    out_weight,
    layer_scale,
    segment_ids,
    pad_mask,
    ln_weight,
    ln_bias,
    fc_weight,
    fc_bias,
    owner,
):
    x = residual_in[0]
    rows_here = x.shape[0]
    n_seq, n_rows = lax.axis_size("seq"), lax.axis_size("rows")
    row = lax.axis_index("rows")
    parts = n_rows // SUBS
    sub, part = lax.div(row, parts), lax.rem(row, parts)
    width = D // parts
    chunk = rows_here // CHUNKS
    merged = chunk // SUBS
    hid = fc_weight.shape[1]

    def over_seq(value, d):
        return lax.ppermute(value, "seq", [(i, i ^ d) for i in range(n_seq)])

    def over_sub(value, d):
        return lax.ppermute(value, "rows", [(i, i ^ (d * parts)) for i in range(n_rows)])

    def over_part(value, d):
        return lax.ppermute(value, "rows", [(i, i ^ d) for i in range(n_rows)])

    def pick(value, index, axis=0):
        return lax.dynamic_index_in_dim(value, index, axis, keepdims=False)

    fence = lax.optimization_barrier

    tokens = reorder(x, chunk)
    cuts = [0, rows_here // 4, rows_here * 3 // 4, rows_here]
    cut = [tokens[: cuts[1]]]
    near, later = fence((over_seq(tokens, 1), tokens))
    cut += [later[low:high] for low, high in zip(cuts[1:], cuts[2:])]
    by_sub = later.reshape(CHUNKS, SUBS, merged, D)
    residual = {0: pick(by_sub, sub, 1)}
    to_send = {d: pick(by_sub, sub ^ d, 1) for d in range(1, SUBS)}
    depth = out_weight.shape[0]
    across = max(1, min(2, depth // 256, parts))
    strip = lax.bitwise_and(part, across - 1) * 2 + lax.bitwise_and(sub, 1)
    size = depth // (2 * across)
    own_strip = lax.dynamic_slice_in_dim(out_weight, strip * size, size, 0)
    group = max(1, min(n_seq, TILE // rows_here))
    projected, squares = {}, {}

    own_id = segment_ids[0, :1]
    leads = [own_id] + [over_seq(own_id, d) for d in range(group, n_seq, group)]
    strips = {(d, 0): over_seq(own_strip, d) for d in range(2, n_seq, 2)}
    far = {d: over_seq(cut[0], d) for d in range(2, n_seq, 2)}
    residual[1] = over_sub(to_send[1], 1)
    residual[2] = over_sub(to_send[2][:1], 2)
    given, given_s = project([later, near], norm_gain, qkv_weight)
    for d in range(2):
        projected[d, 0], squares[d, 0] = given[d], given_s[d]
    state = leads, strips, far, residual, to_send, cut, squares, out_weight
    leads, strips, far, residual, to_send, cut, squares, out_weight = fence(state)

    for i in range(len(cut)):
        coming = {}
        if i + 1 < len(cut):
            coming = {d: over_seq(cut[i + 1], d) for d in range(2, n_seq, 2)}
        arrived = dict(strips)
        for d, k in [key for key in arrived if key[0] % 2 == 0]:
            if k == 0 and i == 0:
                strips[d, 1] = over_sub(arrived[d, 0], 1)
            if k == i and across == 2:
                strips[d, 2 + k] = over_part(arrived[d, k], 1)
            if (d + 1, k) not in strips:
                strips[d + 1, k] = over_seq(arrived[d, k], 1)
        if i == 0:
            residual[3] = over_sub(to_send[3][:1], 3)
        if i == 1:
            out_near = over_seq(out_weight, 1)
        for d in range(2, n_seq, 2):
            far[d + 1] = over_seq(far[d], 1)
        given, given_s = project([far[d] for d in range(2, n_seq)], norm_gain, qkv_weight)
        for d in range(2, n_seq):
            projected[d, i], squares[d, i] = given[d - 2], given_s[d - 2]
        if i + 1 < len(cut):
            state = coming, residual, to_send, cut, squares, out_weight, strips
            far, residual, to_send, cut, squares, out_weight, strips = fence(state)
    plan, pieces = [], []
    for d, i in sorted(projected):
        plan.append((d, cuts[i], projected[d, i].shape[0]))
        pieces.append(projected[d, i])

    here = jnp.concatenate([squares[key] for key in sorted(squares)], axis=1)
    here = jnp.transpose(here.reshape(2, n_seq, rows_here), (1, 0, 2))
    total = here
    for e in range(1, n_seq):
        there = over_seq(here, e)
        total = total + jnp.stack([there[d ^ e] for d in range(n_seq)])
    total = jnp.transpose(total, (1, 0, 2)).reshape(2, n_seq * rows_here)

    sub_ln = lax.dynamic_slice_in_dim(ln_weight, sub * D, D, 0)
    sub_bias = lax.dynamic_slice_in_dim(ln_bias, sub * D, D, 0)
    place = jnp.stack([sub, part])
    relative = np.array([d * parts + e for e in range(parts) for d in range(SUBS)], np.int32)

    places = [(0, 0, 0, 0), (1, 1, 0, 0)]

    def heads_of(j, sums):
        return attend(pieces, plan, rows_here, sums, leads, qk_gain, j * chunk, chunk)

    def gather_heads(heads):
        return [heads[0]] + [over_seq(heads[d], d) for d in range(1, n_seq)]

    def gather_rows(packed):
        return [packed[0]] + [over_sub(packed[d], d) for d in range(1, SUBS)]

    def to_hidden(j, mine):
        own = pad_mask[0, :1]
        return hidden_of(
            places[j], mine, residual, out_weights, strip.reshape(1), layer_scale, own
        )

    def to_normed(hidden, stats):
        known = [stats] + [over_sub(stats, e) for e in range(1, SUBS)]
        *normed, line = norm(hidden, known, sub_ln, sub_bias, part, parts)
        return normed, line

    def over_parts(values):
        return [values[0]] + [over_part(values[e], e) for e in range(1, parts)]

    total, to_send, strips = fence((total, to_send, strips))

    last = {3: over_sub(to_send[3][1:], 3)}
    heads_0 = heads_of(0, total)
    heads_0, total, last, to_send = fence((heads_0, total, last, to_send))

    last[2] = over_sub(to_send[2][1:], 2)
    heads_1 = heads_of(1, total)
    groups_0 = gather_heads(heads_0)
    heads_1, groups_0, last = fence((heads_1, groups_0, last))

    rows_0 = gather_rows(pack(groups_0, sub))
    packed_1 = pack(gather_heads(heads_1), sub)
    rows_0, packed_1 = fence((rows_0, packed_1))

    out_weights = [[out_weight], [out_near]]
    for d in range(2, n_seq):
        out_weights.append([strips[d, k] for k in range(2 * across)])
    residual = [residual[d] for d in range(SUBS)]
    rows_1 = gather_rows(packed_1)
    normed_0, line = to_normed(*to_hidden(0, rows_0))
    normed_0, line, rows_1 = fence((normed_0, line, rows_1))

    slab_0 = over_parts(normed_0)
    residual = [*residual[:2], last[2], last[3]]
    normed_1, _ = to_normed(*to_hidden(1, rows_1))
    slab_0, line, normed_1 = fence((slab_0, line, normed_1))

    slab_1 = over_parts(normed_1)
    waiting = shares_of(slab_0, place, owner, fc_weight)
    slab_1, waiting, line = fence((slab_1, waiting, line))

    units = CHUNKS * HALVES
    by_part, by_sub, outs, own_mask = [], [], [], None
    for tick in range(units + 2):
        new_by_part, new_by_sub = [], []
        if waiting:
            new_by_part = [over_parts(waiting[0])]
            waiting = waiting[1:]
        if tick == 0:
            waiting = waiting + shares_of(slab_1, place, owner, fc_weight)
            own_mask = over_parts([line] * parts)
        if tick == 1:
            masks = jnp.concatenate(own_mask)
            given = (row ^ relative)[:, None] == jnp.arange(n_rows, dtype=jnp.int32)[None, :]
            given = given & (owner[None, :] == row)
            given = jnp.any(given, axis=1)[:, None]
            own_mask = jnp.sum(jnp.where(given, masks, 0.0), axis=0)[:1]
        if by_part:
            summed = add(by_part[0])
            new_by_sub = [[summed[0]] + [over_sub(summed[d], d) for d in range(1, SUBS)]]
        if by_sub:
            outs = outs + [finish(by_sub[0], fc_bias, own_mask)]
        state = waiting, new_by_part, new_by_sub, outs, own_mask
        waiting, by_part, by_sub, outs, own_mask = fence(state)
    return jnp.concatenate(outs, axis=0)[None]


def solution(mesh):
    return jax.shard_map(
        per_device,
        mesh=mesh,
        in_specs=(
            P("rows", "seq", None),
            P(),
            P(None, "seq"),
            P(None, "seq"),
            P("seq", None),
            P(),
            P("rows", "seq"),
            P("rows", "seq"),
            P(),
            P(),
            P("rows", None),
            P(),
            P(),
        ),
        out_specs=P("rows", "seq", None),
        check_vma=False,
    )
```

```python
import functools
import math

import jax
import jax.numpy as jnp
import numpy as np
from jax import lax
from jax.experimental import pallas as pl
from jax.experimental.pallas import tpu as pltpu
from jax.sharding import PartitionSpec as P

D = 3200
HEAD_DIM = 128
HEADS = 16
GRID = 32
TILE = GRID * GRID
SUBS = 4
CHUNKS = 2
HALVES = 2
MIB = 1024 * 1024
BF16 = jnp.bfloat16
F32 = jnp.float32
TINY = pl.CostEstimate(flops=1, bytes_accessed=1, transcendentals=0)


def reorder_kernel(pick_ref, x_ref, out_ref):
    out_ref[...] = jnp.dot(pick_ref[...], x_ref[...], preferred_element_type=F32).astype(BF16)


def reorder(x, chunk):
    lines = chunk // (2 * GRID)
    source = np.arange(chunk).reshape(lines, 2, GRID // 2, 2).transpose(1, 3, 0, 2).reshape(chunk)
    pick = jnp.asarray(np.eye(chunk, dtype=np.float32)[source], BF16)
    return pl.pallas_call(
        reorder_kernel,
        grid=(x.shape[0] // chunk,),
        in_specs=[
            pl.BlockSpec((chunk, chunk), lambda i: (0, 0)),
            pl.BlockSpec((chunk, D), lambda i: (i, 0)),
        ],
        out_specs=pl.BlockSpec((chunk, D), lambda i: (i, 0)),
        out_shape=jax.ShapeDtypeStruct(x.shape, BF16),
        cost_estimate=pl.CostEstimate(
            flops=2 * x.shape[0] * chunk * D, bytes_accessed=4 * x.size, transcendentals=0
        ),
        compiler_params=pltpu.CompilerParams(vmem_limit_bytes=32 * MIB),
        name="reorder",
    )(pick, x)


def qkv_kernel(count, *refs):
    x_refs, gain_ref, w_ref = refs[:count], refs[count], refs[count + 1]
    out_refs = refs[count + 2 : 2 * count + 2]
    sq_refs = refs[2 * count + 2 : 3 * count + 2]
    normed, q_acc, k_acc = refs[3 * count + 2 :]
    head = pl.program_id(0)
    rows = x_refs[0].shape[0]
    step = 64

    @pl.when(head == 0)
    def _():
        for i in range(count):

            @pl.loop(0, rows // step)
            def _(b):
                part = pl.ds(pl.multiple_of(b * step, step), step)
                x = x_refs[i][part, :].astype(F32)
                inv = lax.rsqrt(jnp.mean(x * x, axis=-1, keepdims=True) + 1e-06)
                normed[i, part, :] = (x * inv * gain_ref[...]).astype(BF16)

        q_acc[...] = jnp.zeros_like(q_acc)
        k_acc[...] = jnp.zeros_like(k_acc)

    for i in range(count):
        product = jnp.dot(normed[i], w_ref[...], preferred_element_type=F32)
        out_refs[i][...] = product
        for first in range(0, product.shape[1], 3 * HEAD_DIM):
            q = product[:, first : first + HEAD_DIM]
            k = product[:, first + HEAD_DIM : first + 2 * HEAD_DIM]
            q_acc[i] += q * q
            k_acc[i] += k * k

    @pl.when(head == pl.num_programs(0) - 1)
    def _():
        for i in range(count):
            sq_refs[i][0:1, :] = jnp.sum(q_acc[i].T, axis=0, keepdims=True)
            sq_refs[i][1:2, :] = jnp.sum(k_acc[i].T, axis=0, keepdims=True)


def project(pieces, norm_gain, qkv_weight):
    count = len(pieces)
    rows = pieces[0].shape[0]
    width = qkv_weight.shape[1]
    heads = width // (3 * HEAD_DIM)
    block = 3 * HEAD_DIM * (2 if heads % 2 == 0 else 1)
    results = pl.pallas_call(
        functools.partial(qkv_kernel, count),
        grid=(width // block,),
        in_specs=[pl.BlockSpec((rows, D), lambda h: (0, 0))] * count
        + [
            pl.BlockSpec((1, D), lambda h: (0, 0)),
            pl.BlockSpec((D, block), lambda h: (0, h)),
        ],
        out_specs=[pl.BlockSpec((rows, block), lambda h: (0, h))] * count
        + [pl.BlockSpec((2, rows), lambda h: (0, 0))] * count,
        out_shape=[jax.ShapeDtypeStruct((rows, width), F32)] * count
        + [jax.ShapeDtypeStruct((2, rows), F32)] * count,
        scratch_shapes=[
            pltpu.VMEM((count, rows, D), BF16),
            pltpu.VMEM((count, rows, HEAD_DIM), F32),
            pltpu.VMEM((count, rows, HEAD_DIM), F32),
        ],
        cost_estimate=TINY,
        compiler_params=pltpu.CompilerParams(vmem_limit_bytes=56 * MIB),
        name="qkv",
    )(*pieces, norm_gain.reshape(1, D), qkv_weight)
    return results[:count], results[count:]


def attend_kernel(plan, rows, first, chunk, group, *refs):
    count = len(plan)
    blocks = plan[-1][0] + 1
    groups = blocks // group
    seg_refs, refs = refs[:groups], refs[groups:]
    sq_ref, gain_ref = refs[:2]
    p_refs = refs[2 : 2 + count]
    out_refs = refs[2 + count : 2 + count + blocks]
    q_scale, k_scale, q_all, k_all, v_all = refs[2 + count + blocks :]
    head = pl.program_id(0)
    factor = HEAD_DIM ** (-0.5) * math.log2(math.e)

    @pl.when(head == 0)
    def _():
        inv = lax.rsqrt(sq_ref[...] / (HEADS * HEAD_DIM) + 1e-06)
        for d in range(blocks):
            part = slice(d * rows, (d + 1) * rows)
            k_scale[part, :] = jnp.broadcast_to(inv[1:2, part], (HEAD_DIM, rows)).T
            q_wide = jnp.broadcast_to(inv[0:1, part] * factor, (HEAD_DIM, rows)).T
            q_scale[d * chunk : (d + 1) * chunk, :] = q_wide[first : first + chunk, :]
        v_all[:, HEAD_DIM:] = jnp.ones_like(v_all[:, HEAD_DIM:])

    for (d, start, size), p_ref in zip(plan, p_refs):
        part = slice(d * rows + start, d * rows + start + size)
        k = p_ref[:, HEAD_DIM : 2 * HEAD_DIM]
        k_all[part, :] = (k * k_scale[part, :] * gain_ref[1:2, :]).astype(BF16)
        v_all[part, :HEAD_DIM] = p_ref[:, 2 * HEAD_DIM :].astype(BF16)
        low, high = max(first, start), min(first + chunk, start + size)
        if low < high:
            part = slice(d * chunk + low - first, d * chunk + high - first)
            q = p_ref[low - start : high - start, :HEAD_DIM]
            q_all[part, :] = (q * q_scale[part, :] * gain_ref[0:1, :]).astype(BF16)

    keys = group * rows
    step = min(chunk, 128)

    def attend(d, begin, low, high):
        q = q_all[d * chunk + begin : d * chunk + begin + step, :]
        scores = lax.dot_general(
            q, k_all[low:high, :], (((1,), (1,)), ((), ())), preferred_element_type=F32
        )
        if groups > 2:
            own = d // group
            masked = []
            for g in range(groups):
                part = scores[:, g * keys : (g + 1) * keys]
                if g != own:
                    part = jnp.where(seg_refs[g][0] == seg_refs[own][0], part, -1e30)
                masked.append(part)
            scores = jnp.concatenate(masked, axis=1)
        peak = jnp.max(scores, axis=-1, keepdims=True)
        terms = jnp.exp2(scores - peak).astype(BF16)
        both = jnp.dot(terms, v_all[low:high, :], preferred_element_type=F32)
        out_refs[d][begin : begin + step, :] = (
            both[:, :HEAD_DIM] / both[:, HEAD_DIM:]
        ).astype(BF16)

    def attend_all(d, low, high):
        for begin in range(0, chunk, step):
            attend(d, begin, low, high)

    if groups != 2:
        for d in range(blocks):
            attend_all(d, 0, blocks * rows)
    else:
        joint = seg_refs[0][0] == seg_refs[1][0]

        @pl.when(joint)
        def _():
            for d in range(blocks):
                attend_all(d, 0, blocks * rows)

        @pl.when(jnp.logical_not(joint))
        def _():
            for d in range(blocks):
                own = d // group
                attend_all(d, own * keys, (own + 1) * keys)


def attend(pieces, plan, rows, squares, segments, qk_gain, first, chunk):
    blocks = plan[-1][0] + 1
    width = pieces[0].shape[1]
    heads = width // (3 * HEAD_DIM)
    total = blocks * rows
    group = max(1, min(blocks, TILE // rows))
    return pl.pallas_call(
        functools.partial(attend_kernel, plan, rows, first, chunk, group),
        grid=(heads,),
        in_specs=[pl.BlockSpec(memory_space=pltpu.SMEM)] * len(segments)
        + [
            pl.BlockSpec((2, total), lambda h: (0, 0)),
            pl.BlockSpec((2, HEAD_DIM), lambda h: (0, h)),
        ]
        + [pl.BlockSpec((size, 3 * HEAD_DIM), lambda h: (0, h)) for _, _, size in plan],
        out_specs=[pl.BlockSpec((chunk, HEAD_DIM), lambda h: (0, h))] * blocks,
        out_shape=[jax.ShapeDtypeStruct((chunk, heads * HEAD_DIM), BF16)] * blocks,
        scratch_shapes=[
            pltpu.VMEM((blocks * chunk, HEAD_DIM), F32),
            pltpu.VMEM((total, HEAD_DIM), F32),
            pltpu.VMEM((blocks * chunk, HEAD_DIM), BF16),
            pltpu.VMEM((total, HEAD_DIM), BF16),
            pltpu.VMEM((total, 2 * HEAD_DIM), BF16),
        ],
        cost_estimate=TINY,
        compiler_params=pltpu.CompilerParams(vmem_limit_bytes=56 * MIB),
        name="attend",
    )(*segments, squares, qk_gain, *pieces)


def pack_kernel(sub_ref, *refs):
    outs = refs[-SUBS:]
    rows, width = outs[0].shape[0], refs[0].shape[1]
    for d in range(SUBS):
        part = pl.ds(pl.multiple_of((sub_ref[0] ^ d) * rows, rows), rows)
        for i, ref in enumerate(refs[:-SUBS]):
            outs[d][:, i * width : (i + 1) * width] = ref[part, :]


def pack(groups, sub):
    chunk, width = groups[0].shape
    shape = (chunk // SUBS, width * len(groups))
    vmem = pl.BlockSpec(memory_space=pltpu.VMEM)
    return pl.pallas_call(
        pack_kernel,
        in_specs=[pl.BlockSpec(memory_space=pltpu.SMEM)] + [vmem] * len(groups),
        out_specs=[vmem] * SUBS,
        out_shape=[jax.ShapeDtypeStruct(shape, BF16)] * SUBS,
        compiler_params=pltpu.CompilerParams(vmem_limit_bytes=32 * MIB),
        name="pack",
    )(sub.reshape(1), *groups)


def hidden_kernel(sizes, strip_ref, mask_ref, *refs):
    count = sum(sizes)
    mine_refs, stream_refs = refs[:SUBS], refs[SUBS : 2 * SUBS]
    w_refs = refs[2 * SUBS : 2 * SUBS + count]
    scale_ref, hidden_ref, stats_ref, mine, mean_wide, spread_wide = refs[2 * SUBS + count :]
    rows = mine_refs[0].shape[0]
    depth, block = w_refs[0].shape
    n = pl.program_id(0)

    @pl.when(n == 0)
    def _():
        for i, size in enumerate(sizes):
            width = depth // size
            for k in range(size):
                start = i * depth + (strip_ref[0] ^ k) * width if size > 1 else i * depth
                columns = pl.ds(pl.multiple_of(start, width), width)
                low = i * depth + k * width
                for d in range(SUBS):
                    part = slice(d * rows, (d + 1) * rows)
                    mine[part, low : low + width] = mine_refs[d][:, columns]

    attn = None
    for i, size in enumerate(sizes):
        first = sum(sizes[:i])
        weight = [ref[...] for ref in w_refs[first : first + size]]
        weight = jnp.concatenate(weight, axis=0) if size > 1 else weight[0]
        product = jnp.dot(
            mine[:, i * depth : (i + 1) * depth], weight, preferred_element_type=F32
        )
        attn = product if attn is None else attn + product
    columns = pl.ds(pl.multiple_of(n * block, block), block)
    for d in range(SUBS):
        part = slice(d * rows, (d + 1) * rows)
        stream = stream_refs[d][0].astype(F32)
        hidden_ref[part, columns] = stream + scale_ref[...] * attn[part, :]

    @pl.when(n == pl.num_programs(0) - 1)
    def _():
        for d in range(SUBS):
            part = slice(d * rows, (d + 1) * rows)
            hidden = hidden_ref[part, :]
            mean = jnp.sum(hidden, axis=-1, keepdims=True) / D
            centre = hidden - mean
            spread = jnp.sum(centre * centre, axis=-1, keepdims=True)
            mean_wide[part, :] = jnp.broadcast_to(mean, (rows, 128))
            spread_wide[part, :] = jnp.broadcast_to(spread, (rows, 128))
        stats_ref[0:1, :] = mean_wide[...].T[0:1, :]
        stats_ref[1:2, :] = spread_wide[...].T[0:1, :]
        stats_ref[2:3, :] = jnp.full((1, SUBS * rows), mask_ref[0].astype(F32))


def hidden_of(places, mine, residual, weights, strip, layer_scale, mask):
    rows = mine[0].shape[0]
    count, depth, block = len(weights), weights[0][0].shape[0], D
    sizes = [len(strips) for strips in weights]
    weights = [part for strips in weights for part in strips]
    total = SUBS * rows
    return pl.pallas_call(
        functools.partial(hidden_kernel, sizes),
        grid=(D // block,),
        in_specs=[pl.BlockSpec(memory_space=pltpu.SMEM)] * 2
        + [pl.BlockSpec(mine[0].shape, lambda n: (0, 0))] * SUBS
        + [pl.BlockSpec((1, rows, block), lambda n, j=j: (j, 0, n)) for j in places]
        + [pl.BlockSpec((part.shape[0], block), lambda n: (0, n)) for part in weights]
        + [pl.BlockSpec((1, block), lambda n: (0, n))],
        out_specs=[
            pl.BlockSpec((total, D), lambda n: (0, 0)),
            pl.BlockSpec((3, total), lambda n: (0, 0)),
        ],
        out_shape=[
            jax.ShapeDtypeStruct((total, D), F32),
            jax.ShapeDtypeStruct((3, total), F32),
        ],
        scratch_shapes=[
            pltpu.VMEM((total, count * depth), BF16),
            pltpu.VMEM((total, 128), F32),
            pltpu.VMEM((total, 128), F32),
        ],
        cost_estimate=pl.CostEstimate(
            flops=2 * total * count * depth * D,
            bytes_accessed=2 * count * depth * D + 6 * total * D,
            transcendentals=0,
        ),
        compiler_params=pltpu.CompilerParams(vmem_limit_bytes=48 * MIB),
        name="hidden",
    )(strip, mask, *mine, *residual, *weights, layer_scale.reshape(1, D))


def norm_kernel(parts, part_ref, hidden_ref, *refs):
    stats_refs, (w_ref, b_ref) = refs[:SUBS], refs[SUBS : SUBS + 2]
    outs, line_ref = refs[SUBS + 2 : -1], refs[-1]
    total = hidden_ref.shape[0]
    rows, width = total // SUBS, D // parts
    for e in range(SUBS):
        line_ref[e : e + 1, :] = stats_refs[e][2:3, :128]
    means = [jnp.broadcast_to(ref[0:1, :], (128, total)).T for ref in stats_refs]
    spreads = [jnp.broadcast_to(ref[1:2, :], (128, total)).T for ref in stats_refs]
    for out in outs:
        if out.shape[1] > width:
            out[:, out.shape[1] - 128 :] = jnp.zeros((total, 128), BF16)
    for d in range(SUBS):
        where = [slice((d ^ e) * rows, ((d ^ e) + 1) * rows) for e in range(SUBS)]
        mean = sum(means[e][where[e], :] for e in range(SUBS)) / SUBS
        var = 0.0
        for e in range(SUBS):
            off = means[e][where[e], :] - mean
            var = var + spreads[e][where[e], :] + D * off * off
        inv = lax.rsqrt(var / (SUBS * D) + 1e-05)
        part = slice(d * rows, (d + 1) * rows)
        normed = (hidden_ref[part, :] - mean[:, 0:1]) * inv[:, 0:1] * w_ref[...] + b_ref[...]
        for i in range(parts):
            cut = normed[:, i * width : (i + 1) * width].astype(BF16)
            for e in range(parts):

                @pl.when((part_ref[0] ^ e) == i)
                def _():
                    outs[e][part, :width] = cut


def norm(hidden, stats, weight, bias, part, parts):
    total = hidden.shape[0]
    padded = pl.cdiv(D // parts, 128) * 128
    vmem = pl.BlockSpec(memory_space=pltpu.VMEM)
    return pl.pallas_call(
        functools.partial(norm_kernel, parts),
        in_specs=[pl.BlockSpec(memory_space=pltpu.SMEM)] + [vmem] * (SUBS + 3),
        out_specs=[vmem] * (parts + 1),
        out_shape=[jax.ShapeDtypeStruct((total, padded), BF16)] * parts
        + [jax.ShapeDtypeStruct((SUBS, 128), F32)],
        cost_estimate=TINY,
        compiler_params=pltpu.CompilerParams(vmem_limit_bytes=48 * MIB),
        name="norm",
    )(part.reshape(1), hidden, *stats, weight.reshape(1, D), bias.reshape(1, D))


def shares_kernel(parts, place_ref, owner_ref, *refs):
    slab_refs, w_ref, outs, ordered = refs[:parts], refs[parts], refs[parts + 1 : -1], refs[-1]
    merged, width = slab_refs[0].shape[0] // SUBS, w_ref.shape[0]
    half = merged // HALVES
    size = SUBS * half

    @pl.when(pl.program_id(0) == 0)
    def _():
        sub, part = place_ref[0], place_ref[1]
        for e in range(parts):
            for d in range(SUBS):
                target = owner_ref[(sub ^ d) * parts + (part ^ e)]
                f, g = lax.rem(target, parts) ^ part, lax.div(target, parts) ^ sub
                for h in range(HALVES):
                    start = pl.multiple_of((h * parts + f) * size + g * half, half)
                    low = d * merged + h * half
                    ordered[pl.ds(start, half), :] = slab_refs[e][low : low + half, :width]

    product = jnp.dot(ordered[...], w_ref[...], preferred_element_type=F32)
    for i, out in enumerate(outs):
        out[...] = product[i * size : (i + 1) * size, :].astype(BF16)


def shares_of(slab, place, owner, fc_weight):
    parts = len(slab)
    total = slab[0].shape[0]
    width, hid = fc_weight.shape
    block = 1536
    size = total // HALVES
    outs = pl.pallas_call(
        functools.partial(shares_kernel, parts),
        grid=(hid // block,),
        in_specs=[pl.BlockSpec(memory_space=pltpu.SMEM)] * 2
        + [pl.BlockSpec(slab[0].shape, lambda n: (0, 0))] * parts
        + [pl.BlockSpec((width, block), lambda n: (0, n))],
        out_specs=[pl.BlockSpec((size, block), lambda n: (0, n))] * (HALVES * parts),
        out_shape=[jax.ShapeDtypeStruct((size, hid), BF16)] * (HALVES * parts),
        scratch_shapes=[pltpu.VMEM((parts * total, width), BF16)],
        cost_estimate=pl.CostEstimate(
            flops=2 * parts * total * width * hid,
            bytes_accessed=2 * width * hid + 2 * parts * total * (width + hid),
            transcendentals=0,
        ),
        compiler_params=pltpu.CompilerParams(vmem_limit_bytes=48 * MIB),
        name="shares",
    )(place, owner, *slab, fc_weight)
    return [outs[h * parts : (h + 1) * parts] for h in range(HALVES)]


def add_kernel(count, *refs):
    rows = refs[count].shape[0]
    for d in range(SUBS):
        part = slice(d * rows, (d + 1) * rows)
        total = refs[0][part, :].astype(F32)
        for ref in refs[1:count]:
            total += ref[part, :].astype(F32)
        refs[count + d][...] = total.astype(BF16)


def add(terms):
    rows, hid = terms[0].shape
    block = 1536
    return pl.pallas_call(
        functools.partial(add_kernel, len(terms)),
        grid=(hid // block,),
        in_specs=[pl.BlockSpec((rows, block), lambda n: (0, n))] * len(terms),
        out_specs=[pl.BlockSpec((rows // SUBS, block), lambda n: (0, n))] * SUBS,
        out_shape=[jax.ShapeDtypeStruct((rows // SUBS, hid), BF16)] * SUBS,
        cost_estimate=pl.CostEstimate(
            flops=len(terms) * rows * hid,
            bytes_accessed=2 * (len(terms) + 1) * rows * hid,
            transcendentals=0,
        ),
        compiler_params=pltpu.CompilerParams(vmem_limit_bytes=32 * MIB),
        name="add",
    )(*terms)


def finish_kernel(mask_ref, bias_ref, *refs):
    pre = refs[0][...].astype(F32)
    for ref in refs[1:-1]:
        pre += ref[...].astype(F32)
    pre += bias_ref[...]
    half = 0.5 * pre * (1.0 + lax.erf(pre * math.sqrt(0.5)))
    refs[-1][...] = (half * mask_ref[0]).astype(BF16)


def finish(terms, bias, mask):
    rows, hid = terms[0].shape
    block = 1536
    return pl.pallas_call(
        finish_kernel,
        grid=(hid // block,),
        in_specs=[
            pl.BlockSpec(memory_space=pltpu.SMEM),
            pl.BlockSpec((1, block), lambda n: (0, n)),
        ]
        + [pl.BlockSpec((rows, block), lambda n: (0, n))] * len(terms),
        out_specs=pl.BlockSpec((rows, block), lambda n: (0, n)),
        out_shape=jax.ShapeDtypeStruct((rows, hid), BF16),
        cost_estimate=TINY,
        compiler_params=pltpu.CompilerParams(vmem_limit_bytes=32 * MIB),
        name="finish",
    )(mask, bias.reshape(1, hid), *terms)


def per_device(
    residual_in,
    norm_gain,
    qkv_weight,
    qk_gain,
    out_weight,
    layer_scale,
    segment_ids,
    pad_mask,
    ln_weight,
    ln_bias,
    fc_weight,
    fc_bias,
    owner,
):
    x = residual_in[0]
    rows_here = x.shape[0]
    n_seq, n_rows = lax.axis_size("seq"), lax.axis_size("rows")
    row = lax.axis_index("rows")
    parts = n_rows // SUBS
    sub, part = lax.div(row, parts), lax.rem(row, parts)
    width = D // parts
    chunk = rows_here // CHUNKS
    merged = chunk // SUBS
    hid = fc_weight.shape[1]

    def over_seq(value, d):
        return lax.ppermute(value, "seq", [(i, i ^ d) for i in range(n_seq)])

    def over_sub(value, d):
        return lax.ppermute(value, "rows", [(i, i ^ (d * parts)) for i in range(n_rows)])

    def over_part(value, d):
        return lax.ppermute(value, "rows", [(i, i ^ d) for i in range(n_rows)])

    def pick(value, index, axis=0):
        return lax.dynamic_index_in_dim(value, index, axis, keepdims=False)

    fence = lax.optimization_barrier

    tokens = reorder(x, chunk)
    cuts = [0, rows_here // 4, rows_here * 3 // 4, rows_here]
    cut = [tokens[: cuts[1]]]
    near, later = fence((over_seq(tokens, 1), tokens))
    cut += [later[low:high] for low, high in zip(cuts[1:], cuts[2:])]
    by_sub = later.reshape(CHUNKS, SUBS, merged, D)
    residual = {0: pick(by_sub, sub, 1)}
    to_send = {d: pick(by_sub, sub ^ d, 1) for d in range(1, SUBS)}
    depth = out_weight.shape[0]
    across = max(1, min(2, depth // 256, parts))
    strip = lax.bitwise_and(part, across - 1) * 2 + lax.bitwise_and(sub, 1)
    size = depth // (2 * across)
    own_strip = lax.dynamic_slice_in_dim(out_weight, strip * size, size, 0)
    group = max(1, min(n_seq, TILE // rows_here))
    projected, squares = {}, {}

    own_id = segment_ids[0, :1]
    leads = [own_id] + [over_seq(own_id, d) for d in range(group, n_seq, group)]
    strips = {(d, 0): over_seq(own_strip, d) for d in range(2, n_seq, 2)}
    far = {d: over_seq(cut[0], d) for d in range(2, n_seq, 2)}
    residual[1] = over_sub(to_send[1], 1)
    residual[2] = over_sub(to_send[2][:1], 2)
    given, given_s = project([later, near], norm_gain, qkv_weight)
    for d in range(2):
        projected[d, 0], squares[d, 0] = given[d], given_s[d]
    state = leads, strips, far, residual, to_send, cut, squares, out_weight
    leads, strips, far, residual, to_send, cut, squares, out_weight = fence(state)

    for i in range(len(cut)):
        coming = {}
        if i + 1 < len(cut):
            coming = {d: over_seq(cut[i + 1], d) for d in range(2, n_seq, 2)}
        arrived = dict(strips)
        for d, k in [key for key in arrived if key[0] % 2 == 0]:
            if k == 0 and i == 0:
                strips[d, 1] = over_sub(arrived[d, 0], 1)
            if k == i and across == 2:
                strips[d, 2 + k] = over_part(arrived[d, k], 1)
            if (d + 1, k) not in strips:
                strips[d + 1, k] = over_seq(arrived[d, k], 1)
        if i == 0:
            residual[3] = over_sub(to_send[3][:1], 3)
        if i == 1:
            out_near = over_seq(out_weight, 1)
        for d in range(2, n_seq, 2):
            far[d + 1] = over_seq(far[d], 1)
        given, given_s = project([far[d] for d in range(2, n_seq)], norm_gain, qkv_weight)
        for d in range(2, n_seq):
            projected[d, i], squares[d, i] = given[d - 2], given_s[d - 2]
        if i + 1 < len(cut):
            state = coming, residual, to_send, cut, squares, out_weight, strips
            far, residual, to_send, cut, squares, out_weight, strips = fence(state)
    plan, pieces = [], []
    for d, i in sorted(projected):
        plan.append((d, cuts[i], projected[d, i].shape[0]))
        pieces.append(projected[d, i])

    here = jnp.concatenate([squares[key] for key in sorted(squares)], axis=1)
    here = jnp.transpose(here.reshape(2, n_seq, rows_here), (1, 0, 2))
    total = here
    for e in range(1, n_seq):
        there = over_seq(here, e)
        total = total + jnp.stack([there[d ^ e] for d in range(n_seq)])
    total = jnp.transpose(total, (1, 0, 2)).reshape(2, n_seq * rows_here)

    sub_ln = lax.dynamic_slice_in_dim(ln_weight, sub * D, D, 0)
    sub_bias = lax.dynamic_slice_in_dim(ln_bias, sub * D, D, 0)
    place = jnp.stack([sub, part])
    relative = np.array([d * parts + e for e in range(parts) for d in range(SUBS)], np.int32)

    places = [(0, 0, 0, 0), (1, 1, 0, 0)]

    def heads_of(j, sums):
        return attend(pieces, plan, rows_here, sums, leads, qk_gain, j * chunk, chunk)

    def gather_heads(heads):
        return [heads[0]] + [over_seq(heads[d], d) for d in range(1, n_seq)]

    def gather_rows(packed):
        return [packed[0]] + [over_sub(packed[d], d) for d in range(1, SUBS)]

    def to_hidden(j, mine):
        own = pad_mask[0, :1]
        return hidden_of(
            places[j], mine, residual, out_weights, strip.reshape(1), layer_scale, own
        )

    def to_normed(hidden, stats):
        known = [stats] + [over_sub(stats, e) for e in range(1, SUBS)]
        *normed, line = norm(hidden, known, sub_ln, sub_bias, part, parts)
        return normed, line

    def over_parts(values):
        return [values[0]] + [over_part(values[e], e) for e in range(1, parts)]

    total, to_send, strips = fence((total, to_send, strips))

    last = {3: over_sub(to_send[3][1:], 3)}
    heads_0 = heads_of(0, total)
    heads_0, total, last, to_send = fence((heads_0, total, last, to_send))

    last[2] = over_sub(to_send[2][1:], 2)
    heads_1 = heads_of(1, total)
    groups_0 = gather_heads(heads_0)
    heads_1, groups_0, last = fence((heads_1, groups_0, last))

    rows_0 = gather_rows(pack(groups_0, sub))
    packed_1 = pack(gather_heads(heads_1), sub)
    rows_0, packed_1 = fence((rows_0, packed_1))

    out_weights = [[out_weight], [out_near]]
    for d in range(2, n_seq):
        out_weights.append([strips[d, k] for k in range(2 * across)])
    residual = [residual[d] for d in range(SUBS)]
    rows_1 = gather_rows(packed_1)
    normed_0, line = to_normed(*to_hidden(0, rows_0))
    normed_0, line, rows_1 = fence((normed_0, line, rows_1))

    slab_0 = over_parts(normed_0)
    residual = [*residual[:2], last[2], last[3]]
    normed_1, _ = to_normed(*to_hidden(1, rows_1))
    slab_1 = over_parts(normed_1)
    waiting = shares_of(slab_0, place, owner, fc_weight)
    slab_1, waiting, line = fence((slab_1, waiting, line))

    units = CHUNKS * HALVES
    by_part, by_sub, outs, own_mask = [], [], [], None
    for tick in range(units + 2):
        new_by_part, new_by_sub = [], []
        if waiting:
            new_by_part = [over_parts(waiting[0])]
            waiting = waiting[1:]
        if tick == 0:
            waiting = waiting + shares_of(slab_1, place, owner, fc_weight)
            own_mask = over_parts([line] * parts)
        if tick == 1:
            masks = jnp.concatenate(own_mask)
            given = (row ^ relative)[:, None] == jnp.arange(n_rows, dtype=jnp.int32)[None, :]
            given = given & (owner[None, :] == row)
            given = jnp.any(given, axis=1)[:, None]
            own_mask = jnp.sum(jnp.where(given, masks, 0.0), axis=0)[:1]
        if by_part:
            summed = add(by_part[0])
            new_by_sub = [[summed[0]] + [over_sub(summed[d], d) for d in range(1, SUBS)]]
        if by_sub:
            outs = outs + [finish(by_sub[0], fc_bias, own_mask)]
        state = waiting, new_by_part, new_by_sub, outs, own_mask
        waiting, by_part, by_sub, outs, own_mask = fence(state)
    return jnp.concatenate(outs, axis=0)[None]


def solution(mesh):
    return jax.shard_map(
        per_device,
        mesh=mesh,
        in_specs=(
            P("rows", "seq", None),
            P(),
            P(None, "seq"),
            P(None, "seq"),
            P("seq", None),
            P(),
            P("rows", "seq"),
            P("rows", "seq"),
            P(),
            P(),
            P("rows", None),
            P(),
            P(),
        ),
        out_specs=P("rows", "seq", None),
        check_vma=False,
    )
```
